256 devices in a mesh: dp: 16 (over z, core), seq: 16 (over x, y).
Axes of the slice: x: 4, y: 4, z: 8, core: 2. Of those that a mesh axis runs over, the one named last changes fastest.
Arguments:
- ssd_input: bfloat16 [65536, 4096], P(('dp', 'seq')), parts along dimension 0, may hold values from -6 to 6
- gate_input: bfloat16 [65536, 4096], P(('dp', 'seq')), parts along dimension 0, may hold values from -6 to 6
- write_map: bfloat16 [65536, 512], P(('dp', 'seq')), parts along dimension 0, may hold values from -6 to 6
- read_map: bfloat16 [65536, 512], P(('dp', 'seq')), parts along dimension 0, may hold values from -6 to 6
- step_size: float32 [65536, 32], P(('dp', 'seq')), parts along dimension 0, may hold values from 0.002 to 51.2, as said below
- decay_log: float32 [32], replicated, as said below
- skip_gain: float32 [32], replicated, may hold values from 0.5 to 1.5
- norm_gain: bfloat16 [4096], replicated, may hold values from 0.099609375 to 1.8984375
- query_rows: bfloat16 [65536, 2048], P(('dp', 'seq')), parts along dimension 0, may hold values from -30 to 30
- key_rows: bfloat16 [65536, 512], P(('dp', 'seq')), parts along dimension 0, may hold values from -4 to 4
- value_rows: bfloat16 [65536, 512], P(('dp', 'seq')), parts along dimension 0, may hold values from -6 to 6
Outputs:
- ssd_out: bfloat16 [65536, 4096], P(('dp', 'seq')), parts along dimension 0
- attn_out: bfloat16 [65536, 2048], P(('dp', 'seq')), parts along dimension 0
The draws below stay inside these ranges and needn't reach their ends.
There are 16 independent parts, one for each index of `dp`. The reference program is written for one: setup_inputs(seed, part) draws one part's arguments, and reference() takes and returns one part's arrays. A program takes and returns all parts, laid end to end along the dimension named above; an argument that names none is the same for every part. Nothing has to cross between parts.
Inputs may be any that keep to these rules, and one draw needn't show every extreme that they name: `step_size`: positive everywhere. Rates exp(decay_log) lie between 30 / 4096 and about 3.4.
All inputs are finite; a program needn't handle non-finite values.
Results may differ from the reference program's by a relative error of at most 0.0059.
Values may be sent and summed in bfloat16 or wider, within the bound.
No kernel may reach another device: no remote copies, remote signals or barrier semaphores. Data moves between devices by JAX's collectives and lax.ppermute only.
A program may use at most 192 MiB of HBM per device.

```python
import math
import jax
import jax.numpy as jnp
from jax import lax

TOK_DEV = 256
MANUSCRIPT_SPAN = 4096
SSD_HEADS = 32
HEAD_DIM = 128
STATE = 128
GROUPS = 4
SPAN = 128
Q_HEADS = 16
KV_HEADS = 4
ATT_DIM = 128
N_SEQ = 16


def draw_query_rows(key, part):
    key = jax.random.fold_in(key, 11)
    starting_shift = jnp.clip(jax.random.normal(key, (MANUSCRIPT_SPAN, Q_HEADS, ATT_DIM), jnp.float32), -4.0, 4.0)
    return starting_shift.reshape(MANUSCRIPT_SPAN, Q_HEADS * ATT_DIM).astype(jnp.bfloat16)


def draw_key_rows(key, part):
    key = jax.random.fold_in(key, 12)
    starting_shift = jnp.clip(jax.random.normal(key, (MANUSCRIPT_SPAN, KV_HEADS, ATT_DIM), jnp.float32), -4.0, 4.0)
    return starting_shift.reshape(MANUSCRIPT_SPAN, KV_HEADS * ATT_DIM).astype(jnp.bfloat16)


def draw_step_size(key, part):
    key = jax.random.fold_in(key, 21)
    key_a, key_b, lookup_tertile, key_d, key_e, key_f = jax.random.split(key, 6)
    element_indices = jnp.arange(MANUSCRIPT_SPAN)
    rough = jnp.exp(jax.random.uniform(key_a, (MANUSCRIPT_SPAN, SSD_HEADS), jnp.float32, -math.log(2.0), math.log(2.0)))
    spread = jnp.exp(jax.random.uniform(key_b, (MANUSCRIPT_SPAN // 64 + 1, SSD_HEADS), jnp.float32, -math.log(2.0), math.log(2.0)))
    base_steps = 0.01 * rough * spread[element_indices // 64]
    device_count = MANUSCRIPT_SPAN // TOK_DEV
    volley_device = jax.random.randint(lookup_tertile, (), 0, max(device_count // 4, 1))
    device_of = element_indices // TOK_DEV
    drawn_mask = (device_of > volley_device) & (device_of <= volley_device + device_count // 2)
    drawn_steps = 0.002 * jnp.exp(jax.random.uniform(key_e, (MANUSCRIPT_SPAN, SSD_HEADS), jnp.float32, 0.0, math.log(2.0)))
    step_values = jnp.where(drawn_mask[:, None], drawn_steps, base_steps)
    other_slot = jax.random.randint(key_d, (), 0, MANUSCRIPT_SPAN)
    other_size = 0.01 * MANUSCRIPT_SPAN * jax.random.uniform(key_f, (), jnp.float32, 0.8, 1.15)
    step_values = jnp.where((element_indices == other_slot)[:, None], other_size, step_values)
    edge_slot = (volley_device + 1) * TOK_DEV - 1
    step_values = jnp.where((element_indices == edge_slot)[:, None], 0.0125 * MANUSCRIPT_SPAN, step_values)
    return step_values.astype(jnp.float32)


def draw_decay_log(key, part):
    key = jax.random.fold_in(key, 31)
    key_a, key_b, lookup_tertile = jax.random.split(key, 3)
    fast_count = SSD_HEADS // 2
    head_order = jax.random.permutation(key_a, SSD_HEADS)
    fast = head_order < fast_count
    fast_rate = jnp.exp(jax.random.uniform(key_b, (SSD_HEADS,), jnp.float32, math.log(1.0 / 60.0), math.log(1.0 / 30.0))) / 0.01
    slow_rate = jnp.exp(jax.random.uniform(lookup_tertile, (SSD_HEADS,), jnp.float32, math.log(0.3), math.log(0.6))) / (0.01 * MANUSCRIPT_SPAN)
    return jnp.log(jnp.where(fast, fast_rate, slow_rate)).astype(jnp.float32)


def level_of(stream_key, shape, cuts, low, high):
    gain = 1.0
    for axis_at, blocks in cuts:
        heights = jax.random.uniform(jax.random.fold_in(jax.random.fold_in(stream_key, 6), axis_at), (blocks,), jnp.float32, low / len(cuts), high / len(cuts))
        gain = gain * jnp.repeat(jnp.exp(heights), shape[axis_at] // blocks).reshape((-1,) + (1,) * (len(shape) - 1 - axis_at))
    return gain


def normal_values(rng, dims, scale, most, shards=(), kind=jnp.bfloat16):
    values = scale * jax.random.normal(rng, dims, jnp.float32)
    if shards:
        values = values * level_of(rng, dims, shards, -0.22, 0.18)
    return jnp.clip(values, -most, most).astype(kind)


def setup_inputs(seed: int = 0, part: int = 0) -> dict:
    key_list = jax.random.split(jax.random.key(seed), 12)
    own_keys = jax.random.split(jax.random.fold_in(key_list[11], part), 12)
    ssd_input = normal_values(own_keys[0], (MANUSCRIPT_SPAN, SSD_HEADS * HEAD_DIM), 1.0, 6.0, ((0, 16),))
    gate_input = normal_values(own_keys[1], (MANUSCRIPT_SPAN, SSD_HEADS * HEAD_DIM), 1.0, 6.0, ((0, 16),))
    write_map = normal_values(own_keys[2], (MANUSCRIPT_SPAN, GROUPS * STATE), 1.0, 6.0, ((0, 16),))
    read_map = normal_values(own_keys[3], (MANUSCRIPT_SPAN, GROUPS * STATE), 1.0, 6.0, ((0, 16),))
    step_size = draw_step_size(jax.random.fold_in(jax.random.fold_in(key_list[11], part), 71), part)
    decay_log = draw_decay_log(jax.random.fold_in(key_list[11], 71), part)
    skip_gain = jnp.clip(jax.random.uniform(key_list[6], (SSD_HEADS,), jnp.float32, 0.5, 1.5), 0.5, 1.5)
    norm_gain = jnp.clip(1.0 + 0.18 * jax.random.normal(key_list[7], (SSD_HEADS * HEAD_DIM,), jnp.float32), 0.099609375, 1.8984375).astype(jnp.bfloat16)
    query_rows = draw_query_rows(jax.random.fold_in(jax.random.fold_in(key_list[11], part), 71), part)
    key_rows = draw_key_rows(jax.random.fold_in(jax.random.fold_in(key_list[11], part), 71), part)
    value_rows = normal_values(own_keys[10], (MANUSCRIPT_SPAN, KV_HEADS * ATT_DIM), 1.0, 6.0, ((0, 16),))
    return {"ssd_input": ssd_input, "gate_input": gate_input, "write_map": write_map, "read_map": read_map, "step_size": step_size, "decay_log": decay_log, "skip_gain": skip_gain, "norm_gain": norm_gain, "query_rows": query_rows, "key_rows": key_rows, "value_rows": value_rows}


def gated_norm(mixed_out, gate_input, norm_gain):
    row_count = mixed_out.shape[0]
    gated_y = mixed_out * jax.nn.silu(gate_input.astype(jnp.float32))
    grouped = gated_y.reshape(row_count, GROUPS, -1)
    inverse = lax.rsqrt(lax.optimization_barrier(jnp.mean(grouped * grouped, axis=-1, keepdims=True)) + 1e-05)
    normed = (grouped * inverse).reshape(row_count, -1)
    return (normed * norm_gain.astype(jnp.float32)).astype(jnp.bfloat16)

def round_trip(values):
    return lax.optimization_barrier(values.astype(jnp.bfloat16)).astype(jnp.float32)

def ssd_reference(ssd_input, write_map, read_map, step_size, decay_log, skip_gain):
    per_group = SSD_HEADS // GROUPS
    n_spans = MANUSCRIPT_SPAN // SPAN
    decay_rate = (-jnp.exp(decay_log)).reshape(GROUPS, per_group)
    skip_heads = skip_gain.reshape(GROUPS, per_group)
    inputs_x = ssd_input.reshape(n_spans, SPAN, GROUPS, per_group, HEAD_DIM).astype(jnp.float32)
    write_vals = write_map.reshape(n_spans, SPAN, GROUPS, STATE).astype(jnp.float32)
    read_vals = read_map.reshape(n_spans, SPAN, GROUPS, STATE).astype(jnp.float32)
    steps_dt = step_size.reshape(n_spans, SPAN, GROUPS, per_group)
    causal = jnp.tril(jnp.ones((SPAN, SPAN), dtype=bool))
    highest = lax.Precision.HIGHEST

    def one_span(carry_state, pieces):
        span_x, span_w, span_r, span_dt = pieces
        cumulative = jnp.cumsum(span_dt * decay_rate, axis=0)
        log_gap = cumulative[:, None] - cumulative[None, :]
        decay_mat = jnp.where(causal[:, :, None, None], jnp.exp(jnp.minimum(log_gap, 0.0)), 0.0)
        intersection = jnp.einsum('tgn,sgn->tsg', span_r, span_w, precision=highest)
        weights = round_trip(intersection[..., None] * decay_mat * span_dt[None])
        local_y = jnp.einsum('tsgj,sgjp->tgjp', weights, span_x, precision=highest)
        state_read = round_trip(carry_state)
        carried = jnp.einsum('tgn,gjnp->tgjp', span_r, state_read, precision=highest) * jnp.exp(cumulative)[..., None]
        to_end = jnp.exp(cumulative[-1][None] - cumulative) * span_dt
        scaled = round_trip(to_end[..., None] * span_x)
        fresh = jnp.einsum('sgn,sgjp->gjnp', span_w, scaled, precision=highest)
        new_state = jnp.exp(cumulative[-1])[..., None, None] * carry_state + fresh
        return (new_state, local_y + carried + skip_heads[:, :, None] * span_x)
    zero_state = jnp.zeros((GROUPS, per_group, STATE, HEAD_DIM), jnp.float32)
    final_state, outputs = lax.scan(one_span, zero_state, (inputs_x, write_vals, read_vals, steps_dt))
    return outputs.reshape(MANUSCRIPT_SPAN, SSD_HEADS * HEAD_DIM)

def attention_reference(query_rows, key_rows, value_rows):
    group_size = Q_HEADS // KV_HEADS
    queries = query_rows.reshape(MANUSCRIPT_SPAN, KV_HEADS, group_size, ATT_DIM).astype(jnp.float32)
    key_all = key_rows.reshape(MANUSCRIPT_SPAN, KV_HEADS, ATT_DIM).astype(jnp.float32)
    value_all = value_rows.reshape(MANUSCRIPT_SPAN, KV_HEADS, ATT_DIM).astype(jnp.float32)
    key_pos = jnp.arange(MANUSCRIPT_SPAN, dtype=jnp.int32)
    score_scale = ATT_DIM ** (-0.5)

    def one_block(start_row):
        block_q = lax.dynamic_slice_in_dim(queries, start_row, TOK_DEV, 0)
        q_pos = start_row + jnp.arange(TOK_DEV, dtype=jnp.int32)
        scores = jnp.einsum('rhgd,khd->hgrk', block_q, key_all) * score_scale
        visible = key_pos[None, :] <= q_pos[:, None]
        scores = jnp.where(visible, scores, -1e+30)
        row_max = lax.optimization_barrier(jnp.max(scores, axis=-1, keepdims=True))
        exps = jnp.where(visible, jnp.exp(scores - row_max), 0.0)
        weight_sum = lax.optimization_barrier(jnp.sum(exps, axis=-1))
        softmax_w = lax.optimization_barrier(exps.astype(jnp.bfloat16)).astype(jnp.float32)
        context = jnp.einsum('hgrk,khd->rhgd', softmax_w, value_all)
        context = context / jnp.transpose(weight_sum, (2, 0, 1))[..., None]
        return context.reshape(TOK_DEV, -1).astype(jnp.bfloat16)
    starts = jnp.arange(N_SEQ, dtype=jnp.int32) * TOK_DEV
    return lax.map(one_block, starts).reshape(MANUSCRIPT_SPAN, Q_HEADS * ATT_DIM)

def reference(ssd_input, gate_input, write_map, read_map, step_size, decay_log, skip_gain, norm_gain, query_rows, key_rows, value_rows):
    mixed_out = ssd_reference(ssd_input, write_map, read_map, step_size, decay_log, skip_gain)
    ssd_out = gated_norm(mixed_out, gate_input, norm_gain)
    attn_out = attention_reference(query_rows, key_rows, value_rows)
    return (ssd_out, attn_out)
```

```python
import math

import jax
import jax.numpy as jnp
import numpy as np
from jax import lax
from jax.experimental import pallas as pl
from jax.experimental.pallas import tpu as pltpu
from jax.sharding import Mesh, PartitionSpec as P

SSD_HEADS = 32
GROUPS = 4
PER = SSD_HEADS // GROUPS
D = 128
NQ = 4
KV_HEADS = 4
SIDE = 4
SCALE = (D**-0.5) * math.log2(math.e)
LOG2E = math.log2(math.e)
BF = jnp.bfloat16
F32 = jnp.float32
NEG = -1e30
EXTRA = 8


def params(mib=48):
    return pltpu.CompilerParams(vmem_limit_bytes=mib << 20)


def pack_body(at_ref, *refs):
    ins, outs = refs[:8], refs[8:]
    for s in range(SIDE):
        outs[s][:, :D] = ins[s][...]
        outs[s][:, D:] = ins[SIDE + s][...]


def pack_kv(at, k, v):
    rows = k.shape[0]

    def spec(s):
        return pl.BlockSpec((rows, D), lambda g, at: (0, lax.rem(at[0] + s, SIDE)))

    whole = pl.BlockSpec((rows, 2 * D), lambda g, at: (0, 0))
    return pl.pallas_call(
        pack_body,
        grid_spec=pltpu.PrefetchScalarGridSpec(
            num_scalar_prefetch=1,
            grid=(1,),
            in_specs=[spec(s) for s in range(SIDE)] * 2,
            out_specs=[whole] * SIDE,
        ),
        out_shape=[jax.ShapeDtypeStruct((rows, 2 * D), BF)] * SIDE,
        name="pack_kv",
    )(at, *([k] * SIDE), *([v] * SIDE))


def pack_q_body(at_ref, *refs):
    for s in range(SIDE):
        refs[SIDE + s][...] = refs[s][...]


def pack_q(at, q):
    rows, cols = q.shape
    width = cols // SIDE

    def spec(s):
        return pl.BlockSpec((rows, width), lambda g, at: (0, lax.rem(at[0] + s, SIDE)))

    whole = pl.BlockSpec((rows, width), lambda g, at: (0, 0))
    return pl.pallas_call(
        pack_q_body,
        grid_spec=pltpu.PrefetchScalarGridSpec(
            num_scalar_prefetch=1,
            grid=(1,),
            in_specs=[spec(s) for s in range(SIDE)],
            out_specs=[whole] * SIDE,
        ),
        out_shape=[jax.ShapeDtypeStruct((rows, width), BF)] * SIDE,
        name="pack_q",
    )(at, *([q] * SIDE))


def span_sums(log_decay, span):
    row = lax.rem(lax.broadcasted_iota(jnp.int32, log_decay.shape, 0), span)
    step = 1
    while step < span:
        moved = pltpu.roll(log_decay, step, 0)
        log_decay = log_decay + jnp.where(row >= step, moved, 0.0)
        step *= 2
    return log_decay


def state_body(at_ref, x_ref, w_ref, dt_ref, rate_ref, *rest):
    outs, first_ref, (to_end, total) = rest[:SIDE], rest[SIDE], rest[SIDE + 1 :]
    s = pl.program_id(0)
    rows = dt_ref.shape[0]
    half = rows // 2
    group = lax.rem(at_ref[1] + s, SIDE)

    @pl.when(s == 0)
    def _():
        dt = dt_ref[...]
        sums = span_sums(dt * (-jnp.exp(rate_ref[...])), half)
        ends = jnp.concatenate(
            [jnp.broadcast_to(sums[half * c + half - 1 : half * c + half], (half, SSD_HEADS)) for c in range(2)],
            axis=0,
        )
        to_end[...] = jnp.exp(ends - sums) * dt
        total[0:8, :] = ends[half : half + 8]
        total[8:16, :] = ends[:8] + ends[half : half + 8]

    for g in range(GROUPS):

        @pl.when(group == g)
        def _():
            scaled, last, decays = [], [], []
            for j in range(PER):
                h = g * PER + j
                scaled.append(
                    (to_end[:, h : h + 1] * x_ref[:, j * D : (j + 1) * D].astype(F32)).astype(BF)
                )
                last.append(jnp.broadcast_to(total[0:1, h : h + 1], (1, D)))
                decays.append(jnp.broadcast_to(total[8:16, h : h + 1], (8, D)))
            scaled = jnp.concatenate(scaled, axis=1)
            first, second = [
                lax.dot_general(
                    w_ref[c * half : (c + 1) * half, :],
                    scaled[c * half : (c + 1) * half],
                    (((0,), (0,)), ((), ())),
                    preferred_element_type=F32,
                )
                for c in range(2)
            ]
            first_ref[0] = first
            state = jnp.exp(jnp.concatenate(last, axis=1)) * first + second
            decay = jnp.concatenate(decays, axis=1)
            for t in range(SIDE):

                @pl.when(s == t)
                def _():
                    outs[t][:D, :] = state
                    outs[t][D:, :] = decay


def local_states(at, x, w, dt, rate):
    rows = x.shape[0]
    width = PER * D
    return pl.pallas_call(
        state_body,
        grid_spec=pltpu.PrefetchScalarGridSpec(
            num_scalar_prefetch=1,
            grid=(SIDE,),
            in_specs=[
                pl.BlockSpec((rows, width), lambda s, at: (0, lax.rem(at[1] + s, SIDE))),
                pl.BlockSpec((rows, D), lambda s, at: (0, lax.rem(at[1] + s, SIDE))),
                pl.BlockSpec((rows, SSD_HEADS), lambda s, at: (0, 0)),
                pl.BlockSpec((1, SSD_HEADS), lambda s, at: (0, 0)),
            ],
            out_specs=[pl.BlockSpec((D + EXTRA, width), lambda s, at: (0, 0))] * SIDE
            + [pl.BlockSpec((1, D, width), lambda s, at: (s, 0, 0))],
            scratch_shapes=[pltpu.VMEM((rows, SSD_HEADS), F32), pltpu.VMEM((16, SSD_HEADS), F32)],
        ),
        out_shape=[jax.ShapeDtypeStruct((D + EXTRA, width), F32)] * SIDE
        + [jax.ShapeDtypeStruct((SIDE, D, width), F32)],
        compiler_params=params(),
        name="local_states",
    )(at, x, w, dt, rate)


def flag(condition):
    return jnp.where(condition, 1.0, 0.0).astype(F32)


def row_total_body(at_ref, *refs):
    ins, outs, total = refs[:SIDE], refs[SIDE : 2 * SIDE], refs[2 * SIDE]
    x, y = at_ref[0], at_ref[1]
    place = [lax.rem(y - s + SIDE, SIDE) for s in range(SIDE)]
    logs = [ref[D : D + 1, :] for ref in ins]
    value = None
    for s in range(SIDE):
        later = sum(flag(place[u] > place[s]) * logs[u] for u in range(SIDE) if u != s)
        term = ins[s][:D, :] * jnp.exp(later)
        value = term if value is None else value + term
    total[:D, :] = value
    total[D:, :] = jnp.broadcast_to(logs[0] + logs[1] + logs[2] + logs[3], (EXTRA, value.shape[1]))
    width = value.shape[1] // SIDE
    for s in range(SIDE):
        begin = pl.multiple_of(lax.rem(x + s, SIDE) * width, width)
        outs[s][...] = total[:, pl.ds(begin, width)]


def row_total(at, states):
    rows, width = states[0].shape
    return pl.pallas_call(
        row_total_body,
        in_specs=[pl.BlockSpec(memory_space=pltpu.SMEM)] + [pl.BlockSpec(memory_space=pltpu.VMEM)] * SIDE,
        out_specs=[pl.BlockSpec(memory_space=pltpu.VMEM)] * SIDE,
        out_shape=[jax.ShapeDtypeStruct((rows, width // SIDE), F32)] * SIDE,
        scratch_shapes=[pltpu.VMEM((rows, width), F32)],
        compiler_params=params(),
        name="row_total",
    )(at, *states)


def entering_body(at_ref, *refs):
    ins, outs = refs[:SIDE], refs[SIDE:]
    prefixes(at_ref[0], ins, outs, None)


def prefixes(mine, ins, outs, entering):
    place = [lax.rem(mine - s + SIDE, SIDE) for s in range(SIDE)]
    logs = [ref[D : D + 1, :] for ref in ins]
    for t in range(SIDE):
        if entering is None:
            state = jnp.zeros((D, ins[0].shape[1]), F32)
        else:
            before = sum(flag(place[u] < place[t]) * logs[u] for u in range(SIDE) if u != t)
            state = jnp.exp(before) * entering
        for s in range(SIDE):
            if s == t:
                continue
            gap = sum(
                flag((place[u] > place[s]) & (place[u] < place[t])) * logs[u]
                for u in range(SIDE)
                if u != t and u != s
            )
            state = state + (flag(place[s] < place[t]) * jnp.exp(gap)) * ins[s][:D, :]
        outs[t][...] = state


def entering_rows(at, totals):
    width = totals[0].shape[1]
    return pl.pallas_call(
        entering_body,
        in_specs=[pl.BlockSpec(memory_space=pltpu.SMEM)] + [pl.BlockSpec(memory_space=pltpu.VMEM)] * SIDE,
        out_specs=[pl.BlockSpec(memory_space=pltpu.VMEM)] * SIDE,
        out_shape=[jax.ShapeDtypeStruct((D, width), F32)] * SIDE,
        compiler_params=params(),
        name="entering_rows",
    )(at, *totals)


def starts_body(at_ref, *refs):
    ins, pieces = refs[:SIDE], refs[SIDE : 2 * SIDE]
    outs, whole = refs[2 * SIDE : 3 * SIDE], refs[3 * SIDE]
    width = pieces[0].shape[1]
    for s in range(SIDE):
        begin = pl.multiple_of(lax.rem(at_ref[0] + s, SIDE) * width, width)
        whole[:, pl.ds(begin, width)] = pieces[s][...]
    prefixes(at_ref[1], ins, outs, whole[...])


def start_states(at, states, entering):
    width = states[0].shape[1]
    return pl.pallas_call(
        starts_body,
        in_specs=[pl.BlockSpec(memory_space=pltpu.SMEM)]
        + [pl.BlockSpec(memory_space=pltpu.VMEM)] * (2 * SIDE),
        out_specs=[pl.BlockSpec(memory_space=pltpu.VMEM)] * SIDE,
        out_shape=[jax.ShapeDtypeStruct((D, width), F32)] * SIDE,
        scratch_shapes=[pltpu.VMEM((D, width), F32)],
        compiler_params=params(),
        name="start_states",
    )(at, *states, *entering)


def ssd_body(
    at_ref, x_ref, gate_ref, w_ref, r_ref, dt_ref, rate_ref, skip_ref, gain_ref, first_ref, *rest
):
    starts, out_ref, (cum, cum_t, ends, gated) = rest[:SIDE], rest[SIDE], rest[SIDE + 1 :]
    s = pl.program_id(0)
    rows = dt_ref.shape[0]
    half = rows // 2
    group = lax.rem(at_ref[1] + s, SIDE)

    @pl.when(s == 0)
    def _():
        dt = dt_ref[...]
        sums = span_sums(dt * (-jnp.exp(rate_ref[...])), half)
        cum[...] = sums * LOG2E
        cum_t[...] = jnp.transpose((sums - jnp.log(dt)) * LOG2E)
        ends[...] = jnp.broadcast_to(sums[half - 1 : half], ends.shape)

    row = lax.broadcasted_iota(jnp.int32, (half, half), 0)
    col = lax.broadcasted_iota(jnp.int32, (half, half), 1)
    causal = col <= row
    spans = [slice(c * half, (c + 1) * half) for c in range(2)]
    pairs = [
        lax.dot_general(
            r_ref[span, :], w_ref[span, :], (((1,), (1,)), ((), ())), preferred_element_type=F32
        )
        for span in spans
    ]

    for g in range(GROUPS):

        @pl.when(group == g)
        def _():
            decay = jnp.exp(
                jnp.concatenate(
                    [
                        jnp.broadcast_to(ends[0:1, g * PER + j : g * PER + j + 1], (1, D))
                        for j in range(PER)
                    ],
                    axis=1,
                )
            )
            for t in range(SIDE):

                @pl.when(s == t)
                def _():
                    start = starts[t][...]
                    gated[spans[0], :] = jnp.dot(
                        r_ref[spans[0], :], start.astype(BF), preferred_element_type=F32
                    )
                    gated[spans[1], :] = jnp.dot(
                        r_ref[spans[1], :],
                        (decay * start + first_ref[0]).astype(BF),
                        preferred_element_type=F32,
                    )

            square = jnp.zeros((rows, D), F32)
            for j in range(PER):
                h = g * PER + j
                lanes = slice(j * D, (j + 1) * D)
                down = jnp.broadcast_to(cum[:, h : h + 1], (rows, D))
                x = x_ref[:, lanes]
                mixed = []
                for c, span in enumerate(spans):
                    weights = pairs[c] * jnp.exp2(down[span] - cum_t[h : h + 1, span])
                    weights = jnp.where(causal, weights, 0.0).astype(BF)
                    mixed.append(jnp.dot(weights, x[span], preferred_element_type=F32))
                mixed = jnp.concatenate(mixed, axis=0)
                mixed = mixed + jnp.exp2(down) * gated[:, lanes] + skip_ref[0, h] * x.astype(F32)
                gate = gate_ref[:, lanes].astype(F32)
                value = mixed * (gate * (0.5 + 0.5 * jnp.tanh(0.5 * gate)))
                gated[:, lanes] = value
                square = square + value * value
            mean = jnp.sum(square, axis=1, keepdims=True) * (1.0 / (PER * D))
            inverse = lax.rsqrt(mean + 1e-05)
            for j in range(PER):
                lanes = slice(j * D, (j + 1) * D)
                out_ref[:, lanes] = (
                    gated[:, lanes] * inverse * gain_ref[:, lanes].astype(F32)
                ).astype(BF)


def ssd_out_of(at, x, gate, w, r, dt, rate, skip, gain, first, starts):
    rows = x.shape[0]
    width = PER * D

    def turned(s, at):
        return (0, lax.rem(at[1] + s, SIDE))

    def fixed(s, at):
        return (0, 0)

    return pl.pallas_call(
        ssd_body,
        grid_spec=pltpu.PrefetchScalarGridSpec(
            num_scalar_prefetch=1,
            grid=(SIDE,),
            in_specs=[
                pl.BlockSpec((rows, width), turned),
                pl.BlockSpec((rows, width), turned),
                pl.BlockSpec((rows, D), turned),
                pl.BlockSpec((rows, D), turned),
                pl.BlockSpec((rows, SSD_HEADS), fixed),
                pl.BlockSpec((1, SSD_HEADS), fixed),
                pl.BlockSpec(memory_space=pltpu.SMEM),
                pl.BlockSpec((1, width), turned),
                pl.BlockSpec((1, D, width), lambda s, at: (s, 0, 0)),
            ]
            + [pl.BlockSpec((D, width), fixed)] * SIDE,
            out_specs=pl.BlockSpec((rows, width), turned),
            scratch_shapes=[
                pltpu.VMEM((rows, SSD_HEADS), F32),
                pltpu.VMEM((SSD_HEADS, rows), F32),
                pltpu.VMEM((8, SSD_HEADS), F32),
                pltpu.VMEM((rows, width), F32),
            ],
        ),
        out_shape=jax.ShapeDtypeStruct(x.shape, BF),
        compiler_params=params(),
        name="ssd_out",
    )(at, x, gate, w, r, dt, rate, skip, gain, first, *starts)


def attn_body(qi_ref, ci_ref, at_ref, q_ref, *rest):
    parts, o_ref, (qs, kk, va, acc, top) = rest[:SIDE], rest[SIDE], rest[SIDE + 1 :]
    step = pl.program_id(0)
    qi = qi_ref[step]
    ci = ci_ref[step]
    x = at_ref[0]
    y = at_ref[1]
    rows = q_ref.shape[0]
    keys = SIDE * rows

    @pl.when(step == 0)
    def _():
        for u in range(SIDE):
            for c in range(SIDE):
                source = slice(c * rows, (c + 1) * rows)
                to = slice(c * keys + u * rows, c * keys + (u + 1) * rows)
                kk[to, :D] = parts[u][source, :D]
                kk[to, D:] = parts[u][source, :D]
                va[to, :D] = parts[u][source, D:]
        va[:, D:] = jnp.ones((SIDE * keys, D), BF)

    @pl.when(ci == 0)
    def _():
        for h in range(NQ):
            q = q_ref[:, h * D : (h + 1) * D].astype(F32) * SCALE
            hi = q.astype(BF)
            qs[h * rows : (h + 1) * rows, :D] = hi
            qs[h * rows : (h + 1) * rows, D:] = (q - hi.astype(F32)).astype(BF)
        acc[...] = jnp.zeros_like(acc)
        top[...] = jnp.full_like(top, NEG)

    slot = lax.rem(x - ci + SIDE, SIDE)
    where = pl.ds(pl.multiple_of(slot * keys, keys), keys)

    def run(masked):
        kc = kk.at[where, :]
        vc = va.at[where, :]
        if masked:
            key = lax.broadcasted_iota(jnp.int32, (rows, rows), 1)
            query = lax.broadcasted_iota(jnp.int32, (rows, rows), 0)
            ahead = key - query

        def scores(h):
            mine = qs[h * rows : (h + 1) * rows, :]
            pieces = []
            for u in range(SIDE):
                piece = lax.dot_general(
                    mine,
                    kc[u * rows : (u + 1) * rows, :],
                    (((1,), (1,)), ((), ())),
                    preferred_element_type=F32,
                )
                if masked:
                    behind = (y - lax.rem(y - u + SIDE, SIDE)) * rows
                    piece = jnp.where(ahead <= behind, piece, NEG)
                pieces.append(piece)
            return jnp.concatenate(pieces, axis=1)

        now = scores(0)
        for h in range(NQ):
            following = scores(h + 1) if h + 1 < NQ else None
            mine = slice(h * rows, (h + 1) * rows)
            old = top[mine, :]
            new = jnp.maximum(old, jnp.max(now, axis=1, keepdims=True))
            factor = jnp.exp2(old - new)
            weights = jnp.exp2(now - new[:, :1]).astype(BF)
            top[mine, :] = new
            out = acc[mine, :] * jnp.concatenate([factor, factor], axis=1)
            for u in range(SIDE):
                out = out + jnp.dot(
                    weights[:, u * rows : (u + 1) * rows],
                    vc[u * rows : (u + 1) * rows, :],
                    preferred_element_type=F32,
                )
            acc[mine, :] = out
            now = following

    @pl.when(ci < qi)
    def _():
        run(False)

    @pl.when(ci == qi)
    def _():
        run(True)
        for h in range(NQ):
            mine = slice(h * rows, (h + 1) * rows)
            o_ref[:, h * D : (h + 1) * D] = (acc[mine, :D] / acc[mine, D:]).astype(BF)


def attention(at, q, parts):
    rows = q.shape[0] // SIDE
    width = q.shape[1]
    keys = parts[0].shape[0]
    order = [(a, c) for a in range(SIDE) for c in range(a + 1)]
    qi = np.array([a for a, _ in order], np.int32)
    ci = np.array([c for _, c in order], np.int32)

    def turned(step, qi, ci, at):
        return (lax.rem(at[0] - qi[step] + SIDE, SIDE), 0)

    return pl.pallas_call(
        attn_body,
        grid_spec=pltpu.PrefetchScalarGridSpec(
            num_scalar_prefetch=3,
            grid=(len(order),),
            in_specs=[pl.BlockSpec((rows, width), turned)]
            + [pl.BlockSpec((keys, 2 * D), lambda step, qi, ci, at: (0, 0))] * SIDE,
            out_specs=pl.BlockSpec((rows, width), turned),
            scratch_shapes=[
                pltpu.VMEM((NQ * rows, 2 * D), BF),
                pltpu.VMEM((SIDE * keys, 2 * D), BF),
                pltpu.VMEM((SIDE * keys, 2 * D), BF),
                pltpu.VMEM((NQ * rows, 2 * D), F32),
                pltpu.VMEM((NQ * rows, D), F32),
            ],
        ),
        out_shape=jax.ShapeDtypeStruct(q.shape, BF),
        compiler_params=params(),
        name="attention",
    )(jnp.asarray(qi), jnp.asarray(ci), at, q, *parts)


def unpack_body(at_ref, *refs):
    ins, out = refs[:SIDE], refs[SIDE]
    s = pl.program_id(0)
    for t in range(SIDE):

        @pl.when(s == t)
        def _():
            out[...] = ins[t][...]


def unpack(at, pieces):
    rows, width = pieces[0].shape
    return pl.pallas_call(
        unpack_body,
        grid_spec=pltpu.PrefetchScalarGridSpec(
            num_scalar_prefetch=1,
            grid=(SIDE,),
            in_specs=[pl.BlockSpec((rows, width), lambda s, at: (0, 0))] * SIDE,
            out_specs=pl.BlockSpec((rows, width), lambda s, at: (0, lax.rem(at[0] + s, SIDE))),
        ),
        out_shape=jax.ShapeDtypeStruct((rows, SIDE * width), BF),
        name="unpack",
    )(at, *pieces)


def shifted(value, axis, by):
    return lax.ppermute(value, axis, [(i, (i + by) % SIDE) for i in range(SIDE)])


def exchange(pieces, axis, sign):
    return [pieces[0]] + [shifted(pieces[s], axis, sign * s) for s in range(1, SIDE)]


def gather_ring(own, axis):
    middle = own.shape[0] // 2
    before = shifted(own, axis, 1)
    after = shifted(own, axis, -1)
    top = shifted(before[:middle], axis, 1)
    bottom = shifted(after[middle:], axis, -1)
    return [own, before, jnp.concatenate([top, bottom], axis=0), after]


def local(
    ssd_input, gate_input, write_map, read_map, step_size, decay_log, skip_gain, norm_gain,
    query_rows, key_rows, value_rows,
):
    at = jnp.stack([lax.axis_index("x"), lax.axis_index("y")]).astype(jnp.int32)
    rate = decay_log.reshape(1, -1)
    skip = skip_gain.reshape(1, -1)
    gain = norm_gain.reshape(1, -1)
    kv = exchange(pack_kv(at, key_rows, value_rows), "x", 1)
    *states, first = local_states(at, ssd_input, write_map, step_size, rate)
    states = exchange(states, "y", 1)
    queries = exchange(pack_q(at, query_rows), "x", 1)
    own = jnp.concatenate(kv, axis=0)
    parts = gather_ring(own, "y")
    totals = exchange(row_total(at, states), "x", 1)
    entering = exchange(entering_rows(at, totals), "x", -1)
    starts = exchange(start_states(at, states, entering), "y", -1)
    q_all = jnp.concatenate(queries, axis=0)
    attended = attention(at, q_all, parts)
    rows = query_rows.shape[0]
    back = exchange([attended[s * rows : (s + 1) * rows] for s in range(SIDE)], "x", -1)
    ssd = ssd_out_of(
        at, ssd_input, gate_input, write_map, read_map, step_size, rate, skip, gain, first, starts
    )
    return (ssd, unpack(at, back))


def solution(mesh):
    grid = Mesh(mesh.devices.reshape(-1, SIDE, SIDE), ("dp", "x", "y"))
    split = P(("dp", "x", "y"), None)
    in_specs = (split,) * 5 + (P(), P(), P()) + (split,) * 3
    return jax.shard_map(
        local, mesh=grid, in_specs=in_specs, out_specs=(split, split), check_vma=False
    )
```

```python
import math

import jax
import jax.numpy as jnp
from jax import lax
from jax.experimental import pallas as pl
from jax.experimental.pallas import tpu as pltpu
from jax.sharding import Mesh, PartitionSpec as P

SSD_HEADS = 32
GROUPS = 4
PER = SSD_HEADS // GROUPS
D = 128
NQ = 4
KV_HEADS = 4
SIDE = 4
SCALE = (D**-0.5) * math.log2(math.e)
LOG2E = math.log2(math.e)
BF = jnp.bfloat16
F32 = jnp.float32
NEG = -1e30
EXTRA = 8


def params(mib=48):
    return pltpu.CompilerParams(vmem_limit_bytes=mib << 20)


def about(us):
    return pl.CostEstimate(
        flops=int(us * 1.0e9), bytes_accessed=int(us * 3.0e6), transcendentals=0
    )


def columns(begin, width):
    return pl.ds(pl.multiple_of(begin * width, D), width)


def pack_body(at_ref, *refs):
    outs = refs[3 * SIDE :]
    for s in range(SIDE):
        outs[s][:, :D] = refs[3 * s][...]
        outs[s][:, D : 2 * D] = refs[3 * s + 1][...]
        outs[s][:, 2 * D :] = refs[3 * s + 2][...]


def pack(at, k, v, q):
    rows, cols = q.shape
    width = cols // SIDE

    def spec(s, width):
        return pl.BlockSpec((rows, width), lambda g, at: (0, lax.rem(at[0] + s, SIDE)))

    return pl.pallas_call(
        pack_body,
        grid_spec=pltpu.PrefetchScalarGridSpec(
            num_scalar_prefetch=1,
            grid=(1,),
            in_specs=[spec(s, w) for s in range(SIDE) for w in (D, D, width)],
            out_specs=[pl.BlockSpec((rows, 2 * D + width), lambda g, at: (0, 0))] * SIDE,
        ),
        out_shape=[jax.ShapeDtypeStruct((rows, 2 * D + width), BF)] * SIDE,
        compiler_params=params(),
        cost_estimate=about(3),
        name="pack",
    )(at, *([k, v, q] * SIDE))


def stack_body(*refs):
    ins, out = refs[:SIDE], refs[SIDE]
    rows = ins[0].shape[0]
    for s in range(SIDE):
        out[s * rows : (s + 1) * rows, :] = ins[s][...]


def stack(pieces):
    rows = pieces[0].shape[0]
    return pl.pallas_call(
        stack_body,
        grid=(1,),
        in_specs=[pl.BlockSpec((rows, 2 * D), lambda g: (0, 0))] * SIDE,
        out_specs=pl.BlockSpec((SIDE * rows, 2 * D), lambda g: (0, 0)),
        out_shape=jax.ShapeDtypeStruct((SIDE * rows, 2 * D), BF),
        compiler_params=params(),
        cost_estimate=about(2),
        name="stack",
    )(*pieces)


def span_sums(log_decay, span):
    row = lax.rem(lax.broadcasted_iota(jnp.int32, log_decay.shape, 0), span)
    step = 1
    while step < span:
        moved = pltpu.roll(log_decay, step, 0)
        log_decay = log_decay + jnp.where(row >= step, moved, 0.0)
        step *= 2
    return log_decay


def state_body(at_ref, x_ref, w_ref, dt_ref, rate_ref, *rest):
    outs, first_ref, (to_end, total) = rest[:SIDE], rest[SIDE], rest[SIDE + 1 :]
    s = pl.program_id(0)
    rows = dt_ref.shape[0]
    half = rows // 2
    group = lax.rem(at_ref[1] + s, SIDE)

    @pl.when(s == 0)
    def _():
        dt = dt_ref[...]
        sums = span_sums(dt * (-jnp.exp(rate_ref[...])), half)
        ends = jnp.concatenate(
            [jnp.broadcast_to(sums[half * c + half - 1 : half * c + half], (half, SSD_HEADS)) for c in range(2)],
            axis=0,
        )
        to_end[...] = jnp.exp(ends - sums) * dt
        total[0:8, :] = ends[half : half + 8]
        total[8:16, :] = ends[:8] + ends[half : half + 8]

    for g in range(GROUPS):

        @pl.when(group == g)
        def _():
            scaled, last, decays = [], [], []
            for j in range(PER):
                h = g * PER + j
                scaled.append(
                    (to_end[:, h : h + 1] * x_ref[:, j * D : (j + 1) * D].astype(F32)).astype(BF)
                )
                last.append(jnp.broadcast_to(total[0:1, h : h + 1], (1, D)))
                decays.append(jnp.broadcast_to(total[8:16, h : h + 1], (8, D)))
            scaled = jnp.concatenate(scaled, axis=1)
            first, second = [
                lax.dot_general(
                    w_ref[c * half : (c + 1) * half, :],
                    scaled[c * half : (c + 1) * half],
                    (((0,), (0,)), ((), ())),
                    preferred_element_type=F32,
                )
                for c in range(2)
            ]
            first_ref[0] = first
            state = jnp.exp(jnp.concatenate(last, axis=1)) * first + second
            decay = jnp.concatenate(decays, axis=1)
            for t in range(SIDE):

                @pl.when(s == t)
                def _():
                    outs[t][:D, :] = state
                    outs[t][D:, :] = decay


def local_states(at, x, w, dt, rate):
    rows = x.shape[0]
    width = PER * D
    return pl.pallas_call(
        state_body,
        grid_spec=pltpu.PrefetchScalarGridSpec(
            num_scalar_prefetch=1,
            grid=(SIDE,),
            in_specs=[
                pl.BlockSpec((rows, width), lambda s, at: (0, lax.rem(at[1] + s, SIDE))),
                pl.BlockSpec((rows, D), lambda s, at: (0, lax.rem(at[1] + s, SIDE))),
                pl.BlockSpec((rows, SSD_HEADS), lambda s, at: (0, 0)),
                pl.BlockSpec((1, SSD_HEADS), lambda s, at: (0, 0)),
            ],
            out_specs=[pl.BlockSpec((D + EXTRA, width), lambda s, at: (0, 0))] * SIDE
            + [pl.BlockSpec((1, D, width), lambda s, at: (s, 0, 0))],
            scratch_shapes=[pltpu.VMEM((rows, SSD_HEADS), F32), pltpu.VMEM((16, SSD_HEADS), F32)],
        ),
        out_shape=[jax.ShapeDtypeStruct((D + EXTRA, width), F32)] * SIDE
        + [jax.ShapeDtypeStruct((SIDE, D, width), F32)],
        compiler_params=params(),
        cost_estimate=about(6),
        name="local_states",
    )(at, x, w, dt, rate)


def flag(condition):
    return jnp.where(condition, 1.0, 0.0).astype(F32)


def row_total_body(at_ref, *refs):
    ins, outs, total = refs[:SIDE], refs[SIDE : 2 * SIDE], refs[2 * SIDE]
    x, y = at_ref[0], at_ref[1]
    place = [lax.rem(y - s + SIDE, SIDE) for s in range(SIDE)]
    logs = [ref[D : D + 1, :] for ref in ins]
    value = None
    for s in range(SIDE):
        later = sum(flag(place[u] > place[s]) * logs[u] for u in range(SIDE) if u != s)
        term = ins[s][:D, :] * jnp.exp(later)
        value = term if value is None else value + term
    total[:D, :] = value
    total[D:, :] = jnp.broadcast_to(logs[0] + logs[1] + logs[2] + logs[3], (EXTRA, value.shape[1]))
    width = value.shape[1] // SIDE
    for s in range(SIDE):
        begin = pl.multiple_of(lax.rem(x + s, SIDE) * width, width)
        outs[s][...] = total[:, pl.ds(begin, width)]


def row_total(at, states):
    rows, width = states[0].shape
    return pl.pallas_call(
        row_total_body,
        in_specs=[pl.BlockSpec(memory_space=pltpu.SMEM)] + [pl.BlockSpec(memory_space=pltpu.VMEM)] * SIDE,
        out_specs=[pl.BlockSpec(memory_space=pltpu.VMEM)] * SIDE,
        out_shape=[jax.ShapeDtypeStruct((rows, width // SIDE), F32)] * SIDE,
        scratch_shapes=[pltpu.VMEM((rows, width), F32)],
        compiler_params=params(),
        cost_estimate=about(2),
        name="row_total",
    )(at, *states)


def entering_body(at_ref, *refs):
    ins, outs = refs[:SIDE], refs[SIDE:]
    prefixes(at_ref[0], ins, outs, None)


def prefixes(mine, ins, outs, entering):
    place = [lax.rem(mine - s + SIDE, SIDE) for s in range(SIDE)]
    logs = [ref[D : D + 1, :] for ref in ins]
    for t in range(SIDE):
        if entering is None:
            state = jnp.zeros((D, ins[0].shape[1]), F32)
        else:
            before = sum(flag(place[u] < place[t]) * logs[u] for u in range(SIDE) if u != t)
            state = jnp.exp(before) * entering
        for s in range(SIDE):
            if s == t:
                continue
            gap = sum(
                flag((place[u] > place[s]) & (place[u] < place[t])) * logs[u]
                for u in range(SIDE)
                if u != t and u != s
            )
            state = state + (flag(place[s] < place[t]) * jnp.exp(gap)) * ins[s][:D, :]
        outs[t][...] = state


def entering_rows(at, totals):
    width = totals[0].shape[1]
    return pl.pallas_call(
        entering_body,
        in_specs=[pl.BlockSpec(memory_space=pltpu.SMEM)] + [pl.BlockSpec(memory_space=pltpu.VMEM)] * SIDE,
        out_specs=[pl.BlockSpec(memory_space=pltpu.VMEM)] * SIDE,
        out_shape=[jax.ShapeDtypeStruct((D, width), F32)] * SIDE,
        compiler_params=params(),
        cost_estimate=about(1),
        name="entering_rows",
    )(at, *totals)


def starts_body(at_ref, *refs):
    ins, pieces = refs[:SIDE], refs[SIDE : 2 * SIDE]
    outs, whole = refs[2 * SIDE : 3 * SIDE], refs[3 * SIDE]
    width = pieces[0].shape[1]
    for s in range(SIDE):
        begin = pl.multiple_of(lax.rem(at_ref[0] + s, SIDE) * width, width)
        whole[:, pl.ds(begin, width)] = pieces[s][...]
    prefixes(at_ref[1], ins, outs, whole[...])


def start_states(at, states, entering):
    width = states[0].shape[1]
    return pl.pallas_call(
        starts_body,
        in_specs=[pl.BlockSpec(memory_space=pltpu.SMEM)]
        + [pl.BlockSpec(memory_space=pltpu.VMEM)] * (2 * SIDE),
        out_specs=[pl.BlockSpec(memory_space=pltpu.VMEM)] * SIDE,
        out_shape=[jax.ShapeDtypeStruct((D, width), F32)] * SIDE,
        scratch_shapes=[pltpu.VMEM((D, width), F32)],
        compiler_params=params(),
        cost_estimate=about(2),
        name="start_states",
    )(at, *states, *entering)


def inside_body(at_ref, x_ref, w_ref, r_ref, dt_ref, rate_ref, skip_ref, out_ref, cum, cum_t):
    s = pl.program_id(0)
    rows = dt_ref.shape[0]
    half = rows // 2
    group = lax.rem(at_ref[1] + s, SIDE)

    @pl.when(s == 0)
    def _():
        dt = dt_ref[...]
        sums = span_sums(dt * (-jnp.exp(rate_ref[...])), half)
        cum[...] = sums * LOG2E
        cum_t[...] = jnp.transpose((sums - jnp.log(dt)) * LOG2E)

    row = lax.broadcasted_iota(jnp.int32, (half, half), 0)
    col = lax.broadcasted_iota(jnp.int32, (half, half), 1)
    causal = col <= row
    spans = [slice(c * half, (c + 1) * half) for c in range(2)]
    pairs = [row_dot(r_ref[span, :], w_ref[span, :]) for span in spans]

    for g in range(GROUPS):

        @pl.when(group == g)
        def _():
            for j in range(PER):
                h = g * PER + j
                lanes = slice(j * D, (j + 1) * D)
                for c, span in enumerate(spans):
                    x = x_ref[span, lanes]
                    down = jnp.broadcast_to(cum[span, h : h + 1], (half, half))
                    weights = pairs[c] * jnp.exp2(down - cum_t[h : h + 1, span])
                    weights = jnp.where(causal, weights, 0.0).astype(BF)
                    out_ref[span, lanes] = jnp.dot(
                        weights, x, preferred_element_type=F32
                    ) + skip_ref[0, h] * x.astype(F32)


def inside_spans(at, x, w, r, dt, rate, skip):
    rows = x.shape[0]
    width = PER * D

    def turned(s, at):
        return (0, lax.rem(at[1] + s, SIDE))

    def fixed(s, at):
        return (0, 0)

    return pl.pallas_call(
        inside_body,
        grid_spec=pltpu.PrefetchScalarGridSpec(
            num_scalar_prefetch=1,
            grid=(SIDE,),
            in_specs=[
                pl.BlockSpec((rows, width), turned),
                pl.BlockSpec((rows, D), turned),
                pl.BlockSpec((rows, D), turned),
                pl.BlockSpec((rows, SSD_HEADS), fixed),
                pl.BlockSpec((1, SSD_HEADS), fixed),
                pl.BlockSpec(memory_space=pltpu.SMEM),
            ],
            out_specs=pl.BlockSpec((rows, width), turned),
            scratch_shapes=[
                pltpu.VMEM((rows, SSD_HEADS), F32),
                pltpu.VMEM((SSD_HEADS, rows), F32),
            ],
        ),
        out_shape=jax.ShapeDtypeStruct(x.shape, F32),
        compiler_params=params(),
        cost_estimate=about(6),
        name="inside_spans",
    )(at, x, w, r, dt, rate, skip)


def ssd_body(
    at_ref, inside_ref, gate_ref, r_ref, dt_ref, rate_ref, gain_ref, first_ref, *rest
):
    starts, out_ref, (grown, ends, gated) = rest[:SIDE], rest[SIDE], rest[SIDE + 1 :]
    s = pl.program_id(0)
    rows = dt_ref.shape[0]
    half = rows // 2
    group = lax.rem(at_ref[1] + s, SIDE)
    spans = [slice(c * half, (c + 1) * half) for c in range(2)]

    @pl.when(s == 0)
    def _():
        sums = span_sums(dt_ref[...] * (-jnp.exp(rate_ref[...])), half)
        grown[...] = jnp.exp(sums)
        ends[...] = jnp.broadcast_to(jnp.exp(sums[half - 1 : half]), ends.shape)

    for g in range(GROUPS):

        @pl.when(group == g)
        def _():
            decay = jnp.concatenate(
                [
                    jnp.broadcast_to(ends[0:1, g * PER + j : g * PER + j + 1], (1, D))
                    for j in range(PER)
                ],
                axis=1,
            )
            for t in range(SIDE):

                @pl.when(s == t)
                def _():
                    start = starts[t][...]
                    gated[spans[0], :] = jnp.dot(
                        r_ref[spans[0], :], start.astype(BF), preferred_element_type=F32
                    )
                    gated[spans[1], :] = jnp.dot(
                        r_ref[spans[1], :],
                        (decay * start + first_ref[0]).astype(BF),
                        preferred_element_type=F32,
                    )

            square = jnp.zeros((rows, D), F32)
            for j in range(PER):
                h = g * PER + j
                lanes = slice(j * D, (j + 1) * D)
                mixed = inside_ref[:, lanes] + grown[:, h : h + 1] * gated[:, lanes]
                gate = gate_ref[:, lanes].astype(F32)
                value = mixed * (gate * (0.5 + 0.5 * jnp.tanh(0.5 * gate)))
                gated[:, lanes] = value
                square = square + value * value
            mean = jnp.sum(square, axis=1, keepdims=True) * (1.0 / (PER * D))
            inverse = lax.rsqrt(mean + 1e-05)
            for j in range(PER):
                lanes = slice(j * D, (j + 1) * D)
                out_ref[:, lanes] = (
                    gated[:, lanes] * inverse * gain_ref[:, lanes].astype(F32)
                ).astype(BF)


def ssd_out_of(at, inside, gate, r, dt, rate, gain, first, starts):
    rows = inside.shape[0]
    width = PER * D

    def turned(s, at):
        return (0, lax.rem(at[1] + s, SIDE))

    def fixed(s, at):
        return (0, 0)

    return pl.pallas_call(
        ssd_body,
        grid_spec=pltpu.PrefetchScalarGridSpec(
            num_scalar_prefetch=1,
            grid=(SIDE,),
            in_specs=[
                pl.BlockSpec((rows, width), turned),
                pl.BlockSpec((rows, width), turned),
                pl.BlockSpec((rows, D), turned),
                pl.BlockSpec((rows, SSD_HEADS), fixed),
                pl.BlockSpec((1, SSD_HEADS), fixed),
                pl.BlockSpec((1, width), turned),
                pl.BlockSpec((1, D, width), lambda s, at: (s, 0, 0)),
            ]
            + [pl.BlockSpec((D, width), fixed)] * SIDE,
            out_specs=pl.BlockSpec((rows, width), turned),
            scratch_shapes=[
                pltpu.VMEM((rows, SSD_HEADS), F32),
                pltpu.VMEM((8, SSD_HEADS), F32),
                pltpu.VMEM((rows, width), F32),
            ],
        ),
        out_shape=jax.ShapeDtypeStruct(gate.shape, BF),
        compiler_params=params(),
        cost_estimate=about(8),
        name="ssd_out",
    )(at, inside, gate, r, dt, rate, gain, first, *starts)


def load_queries(q_ref, qs):
    rows = q_ref.shape[0]
    for h in range(NQ):
        q = q_ref[:, (2 + h) * D : (3 + h) * D].astype(F32) * SCALE
        hi = q.astype(BF)
        qs[h * rows : (h + 1) * rows, :D] = hi
        qs[h * rows : (h + 1) * rows, D:] = (q - hi.astype(F32)).astype(BF)


def row_dot(a, b):
    return lax.dot_general(a, b, (((1,), (1,)), ((), ())), preferred_element_type=F32)


def lane_max(scores):
    return jnp.maximum(scores[:, :D], scores[:, D:])


def spread_max(parts):
    most = parts[0]
    for part in parts[1:]:
        most = jnp.maximum(most, part)
    return jnp.broadcast_to(jnp.max(most, axis=1, keepdims=True), most.shape)


def attention_body(at_ref, *rest):
    pieces, parts, outs = rest[:SIDE], rest[SIDE : 2 * SIDE - 1], rest[2 * SIDE - 1 : 3 * SIDE - 1]
    qs, kk, va, acc, top = rest[3 * SIDE - 1 :]
    place = pl.program_id(0)
    x, y = at_ref[0], at_ref[1]
    rows = pieces[0].shape[0]
    keys = SIDE * rows

    @pl.when(place == 0)
    def _():
        for c in range(SIDE):
            for u in range(SIDE):
                if u == 0:
                    source = pieces[c]
                else:
                    source = parts[u - 1].at[c * rows : (c + 1) * rows, :]
                to = slice(c * keys + u * rows, c * keys + (u + 1) * rows)
                kk[to, :D] = source[:, :D]
                kk[to, D:] = source[:, :D]
                va[to, :D] = source[:, D : 2 * D]
        va[:, D:] = jnp.ones((SIDE * keys, D), BF)

    for s in range(SIDE):

        @pl.when(lax.rem(x - place + SIDE, SIDE) == s)
        def _():
            load_queries(pieces[s], qs)

    acc[...] = jnp.zeros_like(acc)
    top[...] = jnp.full_like(top, NEG)

    def chunk(c, newest):
        where = pl.ds(pl.multiple_of(lax.rem(x - c + SIDE, SIDE) * keys, keys), keys)
        kc, vc = kk.at[where, :], va.at[where, :]
        if newest:
            causal = lax.broadcasted_iota(jnp.int32, (rows, rows), 1) <= lax.broadcasted_iota(
                jnp.int32, (rows, rows), 0
            )
            shown = [0.0] + [
                jnp.where(lax.rem(y - u + SIDE, SIDE) > y, NEG, 0.0).astype(F32)
                for u in range(1, SIDE)
            ]

        def scores(h):
            mine = qs[h * rows : (h + 1) * rows, :]
            found = [row_dot(mine, kc[u * rows : (u + 1) * rows, :]) for u in range(SIDE)]
            if newest:
                found[0] = jnp.where(causal, found[0], NEG)
            return found

        now = scores(0)
        for h in range(NQ):
            following = scores(h + 1) if h + 1 < NQ else None
            mine = slice(h * rows, (h + 1) * rows)
            old = top[mine, :]
            most = [lane_max(part) for part in now]
            if newest:
                most = [part + shift for part, shift in zip(most, shown)]
            new = jnp.maximum(old, spread_max(most))
            wide = jnp.concatenate([new] * (rows // D), axis=1)
            factor = jnp.exp2(old - new)
            top[mine, :] = new
            out = acc[mine, :] * jnp.concatenate([factor, factor], axis=1)
            for u in range(SIDE):
                base = wide - shown[u] if newest and u else wide
                weights = jnp.exp2(now[u] - base).astype(BF)
                out = out + jnp.dot(
                    weights, vc[u * rows : (u + 1) * rows, :], preferred_element_type=F32
                )
            acc[mine, :] = out
            now = following

    def older(c, carry):
        chunk(c, False)
        return carry

    lax.fori_loop(0, place, older, 0)
    chunk(place, True)
    for s in range(SIDE):

        @pl.when(lax.rem(x - place + SIDE, SIDE) == s)
        def _():
            for h in range(NQ):
                mine = slice(h * rows, (h + 1) * rows)
                outs[s][:, h * D : (h + 1) * D] = (acc[mine, :D] / acc[mine, D:]).astype(BF)


def attention(at, pieces, parts):
    rows, width = pieces[0].shape
    given = width - 2 * D
    keys = parts[0].shape[0]

    def fixed(place, at):
        return (0, 0)

    return pl.pallas_call(
        attention_body,
        grid_spec=pltpu.PrefetchScalarGridSpec(
            num_scalar_prefetch=1,
            grid=(SIDE,),
            in_specs=[pl.BlockSpec((rows, width), fixed)] * SIDE
            + [pl.BlockSpec((keys, 2 * D), fixed)] * (SIDE - 1),
            out_specs=[pl.BlockSpec((rows, given), fixed)] * SIDE,
            scratch_shapes=[
                pltpu.VMEM((NQ * rows, 2 * D), BF),
                pltpu.VMEM((SIDE * keys, 2 * D), BF),
                pltpu.VMEM((SIDE * keys, 2 * D), BF),
                pltpu.VMEM((NQ * rows, 2 * D), F32),
                pltpu.VMEM((NQ * rows, D), F32),
            ],
        ),
        out_shape=[jax.ShapeDtypeStruct((rows, given), BF)] * SIDE,
        compiler_params=params(),
        cost_estimate=about(18),
        name="attention",
    )(at, *pieces, *parts)


def unpack_body(at_ref, *refs):
    ins, out = refs[:SIDE], refs[SIDE]
    width = ins[0].shape[1]
    for s in range(SIDE):
        out[:, columns(lax.rem(at_ref[0] + s, SIDE), width)] = ins[s][...]


def unpack(at, pieces):
    rows, width = pieces[0].shape
    return pl.pallas_call(
        unpack_body,
        in_specs=[pl.BlockSpec(memory_space=pltpu.SMEM)]
        + [pl.BlockSpec(memory_space=pltpu.VMEM)] * SIDE,
        out_specs=pl.BlockSpec(memory_space=pltpu.VMEM),
        out_shape=jax.ShapeDtypeStruct((rows, SIDE * width), BF),
        compiler_params=params(),
        cost_estimate=about(2),
        name="unpack",
    )(at, *pieces)


def shifted(value, axis, by):
    return lax.ppermute(value, axis, [(i, (i + by) % SIDE) for i in range(SIDE)])


def exchange(pieces, axis, sign):
    return [pieces[0]] + [shifted(pieces[s], axis, sign * s) for s in range(1, SIDE)]


def local(
    ssd_input, gate_input, write_map, read_map, step_size, decay_log, skip_gain, norm_gain,
    query_rows, key_rows, value_rows,
):
    at = jnp.stack([lax.axis_index("x"), lax.axis_index("y")]).astype(jnp.int32)
    rate = decay_log.reshape(1, -1)
    skip = skip_gain.reshape(1, -1)
    gain = norm_gain.reshape(1, -1)
    tie = lax.optimization_barrier
    *states, first = local_states(at, ssd_input, write_map, step_size, rate)
    states = exchange(states, "y", 1)
    pieces = exchange(pack(at, key_rows, value_rows, query_rows), "x", 1)
    inside = inside_spans(at, ssd_input, write_map, read_map, step_size, rate, skip)
    own = stack(pieces)
    middle = own.shape[0] // 2
    before = shifted(own, "y", 1)
    after = shifted(own, "y", -1)
    states, inside = tie((states, inside))
    totals = exchange(row_total(at, states), "x", 1)
    entering = entering_rows(at, totals)
    entering, before, after = tie((entering, before, after))
    far = [shifted(before[:middle], "y", 1), shifted(after[middle:], "y", -1)]
    entering = exchange(entering, "x", -1)
    starts = start_states(at, states, entering)
    starts, pieces = tie((starts, pieces))
    starts = exchange(starts, "y", -1)
    parts = [before, jnp.concatenate(far, axis=0), after]
    back = exchange(attention(at, pieces, parts), "x", -1)
    ssd = ssd_out_of(at, inside, gate_input, read_map, step_size, rate, gain, first, starts)
    ssd, back = tie((ssd, back))
    return (ssd, unpack(at, back))


def solution(mesh):
    grid = Mesh(mesh.devices.reshape(-1, SIDE, SIDE), ("dp", "x", "y"))
    split = P(("dp", "x", "y"), None)
    in_specs = (split,) * 5 + (P(), P(), P()) + (split,) * 3
    return jax.shard_map(
        local, mesh=grid, in_specs=in_specs, out_specs=(split, split), check_vma=False
    )
```

```python
import math

import jax
import jax.numpy as jnp
from jax import lax
from jax.experimental import pallas as pl
from jax.experimental.pallas import tpu as pltpu
from jax.sharding import Mesh, PartitionSpec as P

SSD_HEADS = 32
GROUPS = 4
PER = SSD_HEADS // GROUPS
D = 128
NQ = 4
KV_HEADS = 4
SIDE = 4
SCALE = (D**-0.5) * math.log2(math.e)
LOG2E = math.log2(math.e)
BF = jnp.bfloat16
F32 = jnp.float32
NEG = -1e30
EXTRA = 8


def params(mib=16):
    return pltpu.CompilerParams(vmem_limit_bytes=mib << 20)


def about(us):
    return pl.CostEstimate(
        flops=int(us * 1.0e9), bytes_accessed=int(us * 3.0e6), transcendentals=0
    )


def columns(begin, width):
    return pl.ds(pl.multiple_of(begin * width, D), width)


def pack_body(at_ref, *refs):
    outs = refs[3 * SIDE :]
    for s in range(SIDE):
        outs[s][:, :D] = refs[3 * s][...]
        outs[s][:, D : 2 * D] = refs[3 * s + 1][...]
        outs[s][:, 2 * D :] = refs[3 * s + 2][...]


def pack(at, k, v, q):
    rows, cols = q.shape
    width = cols // SIDE

    def spec(s, width):
        return pl.BlockSpec((rows, width), lambda g, at: (0, lax.rem(at[0] + s, SIDE)))

    return pl.pallas_call(
        pack_body,
        grid_spec=pltpu.PrefetchScalarGridSpec(
            num_scalar_prefetch=1,
            grid=(1,),
            in_specs=[spec(s, w) for s in range(SIDE) for w in (D, D, width)],
            out_specs=[pl.BlockSpec((rows, 2 * D + width), lambda g, at: (0, 0))] * SIDE,
        ),
        out_shape=[jax.ShapeDtypeStruct((rows, 2 * D + width), BF)] * SIDE,
        compiler_params=params(),
        name="pack",
    )(at, *([k, v, q] * SIDE))


def stack_body(*refs):
    ins, out = refs[:SIDE], refs[SIDE]
    rows = ins[0].shape[0]
    for s in range(SIDE):
        out[s * rows : (s + 1) * rows, :] = ins[s][...]


def stack(pieces):
    rows = pieces[0].shape[0]
    return pl.pallas_call(
        stack_body,
        grid=(1,),
        in_specs=[pl.BlockSpec((rows, 2 * D), lambda g: (0, 0))] * SIDE,
        out_specs=pl.BlockSpec((SIDE * rows, 2 * D), lambda g: (0, 0)),
        out_shape=jax.ShapeDtypeStruct((SIDE * rows, 2 * D), BF),
        compiler_params=params(),
        name="stack",
    )(*pieces)


def span_sums(log_decay, span):
    row = lax.rem(lax.broadcasted_iota(jnp.int32, log_decay.shape, 0), span)
    step = 1
    while step < span:
        moved = pltpu.roll(log_decay, step, 0)
        log_decay = log_decay + jnp.where(row >= step, moved, 0.0)
        step *= 2
    return log_decay


def state_body(at_ref, x_ref, w_ref, dt_ref, rate_ref, *rest):
    outs, first_ref, (to_end, total) = rest[:SIDE], rest[SIDE], rest[SIDE + 1 :]
    s = pl.program_id(0)
    rows = dt_ref.shape[1]
    half = rows // 2
    group = lax.rem(at_ref[1] + s, SIDE)

    @pl.when(s == 0)
    def _():
        dt = jnp.transpose(dt_ref[...])
        sums = span_sums(dt * (-jnp.exp(rate_ref[...])), half)
        ends = jnp.concatenate(
            [jnp.broadcast_to(sums[half * c + half - 1 : half * c + half], (half, SSD_HEADS)) for c in range(2)],
            axis=0,
        )
        to_end[...] = jnp.exp(ends - sums) * dt
        total[0:8, :] = ends[half : half + 8]
        total[8:16, :] = ends[:8] + ends[half : half + 8]

    for g in range(GROUPS):

        @pl.when(group == g)
        def _():
            scaled, last, decays = [], [], []
            for j in range(PER):
                h = g * PER + j
                scaled.append(
                    (to_end[:, h : h + 1] * x_ref[:, j * D : (j + 1) * D].astype(F32)).astype(BF)
                )
                last.append(jnp.broadcast_to(total[0:1, h : h + 1], (1, D)))
                decays.append(jnp.broadcast_to(total[8:16, h : h + 1], (8, D)))
            scaled = jnp.concatenate(scaled, axis=1)
            first, second = [
                lax.dot_general(
                    w_ref[c * half : (c + 1) * half, :],
                    scaled[c * half : (c + 1) * half],
                    (((0,), (0,)), ((), ())),
                    preferred_element_type=F32,
                )
                for c in range(2)
            ]
            first_ref[0] = first
            state = jnp.exp(jnp.concatenate(last, axis=1)) * first + second
            decay = jnp.concatenate(decays, axis=1)
            for t in range(SIDE):

                @pl.when(s == t)
                def _():
                    outs[t][:D, :] = state
                    outs[t][D:, :] = decay


def local_states(at, x, w, dt, rate):
    rows = x.shape[0]
    width = PER * D
    return pl.pallas_call(
        state_body,
        grid_spec=pltpu.PrefetchScalarGridSpec(
            num_scalar_prefetch=1,
            grid=(SIDE,),
            in_specs=[
                pl.BlockSpec((rows, width), lambda s, at: (0, lax.rem(at[1] + s, SIDE))),
                pl.BlockSpec((rows, D), lambda s, at: (0, lax.rem(at[1] + s, SIDE))),
                pl.BlockSpec((SSD_HEADS, rows), lambda s, at: (0, 0)),
                pl.BlockSpec((1, SSD_HEADS), lambda s, at: (0, 0)),
            ],
            out_specs=[pl.BlockSpec((D + EXTRA, width), lambda s, at: (0, 0))] * SIDE
            + [pl.BlockSpec((1, D, width), lambda s, at: (s, 0, 0))],
            scratch_shapes=[pltpu.VMEM((rows, SSD_HEADS), F32), pltpu.VMEM((16, SSD_HEADS), F32)],
        ),
        out_shape=[jax.ShapeDtypeStruct((D + EXTRA, width), F32)] * SIDE
        + [jax.ShapeDtypeStruct((SIDE, D, width), F32)],
        compiler_params=params(),
        name="local_states",
    )(at, x, w, dt, rate)


def flag(condition):
    return jnp.where(condition, 1.0, 0.0).astype(F32)


def row_total_body(at_ref, *refs):
    ins, outs, total = refs[:SIDE], refs[SIDE : 2 * SIDE], refs[2 * SIDE]
    x, y = at_ref[0], at_ref[1]
    place = [lax.rem(y - s + SIDE, SIDE) for s in range(SIDE)]
    logs = [ref[D : D + 1, :] for ref in ins]
    value = None
    for s in range(SIDE):
        later = sum(flag(place[u] > place[s]) * logs[u] for u in range(SIDE) if u != s)
        term = ins[s][:D, :] * jnp.exp(later)
        value = term if value is None else value + term
    total[:D, :] = value
    total[D:, :] = jnp.broadcast_to(logs[0] + logs[1] + logs[2] + logs[3], (EXTRA, value.shape[1]))
    width = value.shape[1] // SIDE
    for s in range(SIDE):
        begin = pl.multiple_of(lax.rem(x + s, SIDE) * width, width)
        outs[s][...] = total[:, pl.ds(begin, width)]


def row_total(at, states):
    rows, width = states[0].shape
    return pl.pallas_call(
        row_total_body,
        in_specs=[pl.BlockSpec(memory_space=pltpu.SMEM)] + [pl.BlockSpec(memory_space=pltpu.VMEM)] * SIDE,
        out_specs=[pl.BlockSpec(memory_space=pltpu.VMEM)] * SIDE,
        out_shape=[jax.ShapeDtypeStruct((rows, width // SIDE), F32)] * SIDE,
        scratch_shapes=[pltpu.VMEM((rows, width), F32)],
        compiler_params=params(),
        cost_estimate=about(2),
        name="row_total",
    )(at, *states)


def entering_body(at_ref, *refs):
    ins, outs = refs[:SIDE], refs[SIDE:]
    prefixes(at_ref[0], ins, outs, None)


def prefixes(mine, ins, outs, entering):
    place = [lax.rem(mine - s + SIDE, SIDE) for s in range(SIDE)]
    logs = [ref[D : D + 1, :] for ref in ins]
    for t in range(SIDE):
        if entering is None:
            state = jnp.zeros((D, ins[0].shape[1]), F32)
        else:
            before = sum(flag(place[u] < place[t]) * logs[u] for u in range(SIDE) if u != t)
            state = jnp.exp(before) * entering
        for s in range(SIDE):
            if s == t:
                continue
            gap = sum(
                flag((place[u] > place[s]) & (place[u] < place[t])) * logs[u]
                for u in range(SIDE)
                if u != t and u != s
            )
            state = state + (flag(place[s] < place[t]) * jnp.exp(gap)) * ins[s][:D, :]
        outs[t][...] = state


def entering_rows(at, totals):
    width = totals[0].shape[1]
    return pl.pallas_call(
        entering_body,
        in_specs=[pl.BlockSpec(memory_space=pltpu.SMEM)] + [pl.BlockSpec(memory_space=pltpu.VMEM)] * SIDE,
        out_specs=[pl.BlockSpec(memory_space=pltpu.VMEM)] * SIDE,
        out_shape=[jax.ShapeDtypeStruct((D, width), F32)] * SIDE,
        compiler_params=params(),
        cost_estimate=about(1),
        name="entering_rows",
    )(at, *totals)


def starts_body(at_ref, *refs):
    ins, pieces = refs[:SIDE], refs[SIDE : 2 * SIDE]
    outs, whole = refs[2 * SIDE : 3 * SIDE], refs[3 * SIDE]
    width = pieces[0].shape[1]
    for s in range(SIDE):
        begin = pl.multiple_of(lax.rem(at_ref[0] + s, SIDE) * width, width)
        whole[:, pl.ds(begin, width)] = pieces[s][...]
    prefixes(at_ref[1], ins, outs, whole[...])


def start_states(at, states, entering):
    width = states[0].shape[1]
    return pl.pallas_call(
        starts_body,
        in_specs=[pl.BlockSpec(memory_space=pltpu.SMEM)]
        + [pl.BlockSpec(memory_space=pltpu.VMEM)] * (2 * SIDE),
        out_specs=[pl.BlockSpec(memory_space=pltpu.VMEM)] * SIDE,
        out_shape=[jax.ShapeDtypeStruct((D, width), F32)] * SIDE,
        scratch_shapes=[pltpu.VMEM((D, width), F32)],
        compiler_params=params(),
        cost_estimate=about(2),
        name="start_states",
    )(at, *states, *entering)


def inside_body(at_ref, x_ref, w_ref, r_ref, dt_ref, rate_ref, skip_ref, out_ref, cum, cum_t):
    s = pl.program_id(0)
    rows = dt_ref.shape[1]
    half = rows // 2
    group = lax.rem(at_ref[1] + s, SIDE)

    @pl.when(s == 0)
    def _():
        dt = jnp.transpose(dt_ref[...])
        sums = span_sums(dt * (-jnp.exp(rate_ref[...])), half)
        cum[...] = sums * LOG2E
        cum_t[...] = jnp.transpose((sums - jnp.log(dt)) * LOG2E)

    row = lax.broadcasted_iota(jnp.int32, (half, half), 0)
    col = lax.broadcasted_iota(jnp.int32, (half, half), 1)
    causal = col <= row
    spans = [slice(c * half, (c + 1) * half) for c in range(2)]
    pairs = [row_dot(r_ref[span, :], w_ref[span, :]) for span in spans]

    for g in range(GROUPS):

        @pl.when(group == g)
        def _():
            for j in range(PER):
                h = g * PER + j
                lanes = slice(j * D, (j + 1) * D)
                for c, span in enumerate(spans):
                    x = x_ref[span, lanes]
                    down = jnp.broadcast_to(cum[span, h : h + 1], (half, half))
                    weights = pairs[c] * jnp.exp2(down - cum_t[h : h + 1, span])
                    weights = jnp.where(causal, weights, 0.0).astype(BF)
                    out_ref[span, lanes] = jnp.dot(
                        weights, x, preferred_element_type=F32
                    ) + skip_ref[0, h] * x.astype(F32)


def inside_spans(at, x, w, r, dt, rate, skip):
    rows = x.shape[0]
    width = PER * D

    def turned(s, at):
        return (0, lax.rem(at[1] + s, SIDE))

    def fixed(s, at):
        return (0, 0)

    return pl.pallas_call(
        inside_body,
        grid_spec=pltpu.PrefetchScalarGridSpec(
            num_scalar_prefetch=1,
            grid=(SIDE,),
            in_specs=[
                pl.BlockSpec((rows, width), turned),
                pl.BlockSpec((rows, D), turned),
                pl.BlockSpec((rows, D), turned),
                pl.BlockSpec((SSD_HEADS, rows), fixed),
                pl.BlockSpec((1, SSD_HEADS), fixed),
                pl.BlockSpec(memory_space=pltpu.SMEM),
            ],
            out_specs=pl.BlockSpec((rows, width), turned),
            scratch_shapes=[
                pltpu.VMEM((rows, SSD_HEADS), F32),
                pltpu.VMEM((SSD_HEADS, rows), F32),
            ],
        ),
        out_shape=jax.ShapeDtypeStruct(x.shape, F32),
        compiler_params=params(),
        name="inside_spans",
    )(at, x, w, r, dt, rate, skip)


def ssd_body(
    at_ref, inside_ref, gate_ref, r_ref, dt_ref, rate_ref, gain_ref, first_ref, *rest
):
    starts, out_ref, (grown, ends, gated) = rest[:SIDE], rest[SIDE], rest[SIDE + 1 :]
    s = pl.program_id(0)
    rows = dt_ref.shape[1]
    half = rows // 2
    group = lax.rem(at_ref[1] + s, SIDE)
    spans = [slice(c * half, (c + 1) * half) for c in range(2)]

    @pl.when(s == 0)
    def _():
        sums = span_sums(jnp.transpose(dt_ref[...]) * (-jnp.exp(rate_ref[...])), half)
        grown[...] = jnp.exp(sums)
        ends[...] = jnp.broadcast_to(jnp.exp(sums[half - 1 : half]), ends.shape)

    for g in range(GROUPS):

        @pl.when(group == g)
        def _():
            decay = jnp.concatenate(
                [
                    jnp.broadcast_to(ends[0:1, g * PER + j : g * PER + j + 1], (1, D))
                    for j in range(PER)
                ],
                axis=1,
            )
            for t in range(SIDE):

                @pl.when(s == t)
                def _():
                    start = starts[t][...]
                    gated[spans[0], :] = jnp.dot(
                        r_ref[spans[0], :], start.astype(BF), preferred_element_type=F32
                    )
                    gated[spans[1], :] = jnp.dot(
                        r_ref[spans[1], :],
                        (decay * start + first_ref[0]).astype(BF),
                        preferred_element_type=F32,
                    )

            square = jnp.zeros((rows, D), F32)
            for j in range(PER):
                h = g * PER + j
                lanes = slice(j * D, (j + 1) * D)
                mixed = inside_ref[:, lanes] + grown[:, h : h + 1] * gated[:, lanes]
                gate = gate_ref[:, lanes].astype(F32)
                value = mixed * (gate * (0.5 + 0.5 * jnp.tanh(0.5 * gate)))
                gated[:, lanes] = value
                square = square + value * value
            mean = jnp.sum(square, axis=1, keepdims=True) * (1.0 / (PER * D))
            inverse = lax.rsqrt(mean + 1e-05)
            for j in range(PER):
                lanes = slice(j * D, (j + 1) * D)
                out_ref[:, lanes] = (
                    gated[:, lanes] * inverse * gain_ref[:, lanes].astype(F32)
                ).astype(BF)


def ssd_out_of(at, inside, gate, r, dt, rate, gain, first, starts):
    rows = inside.shape[0]
    width = PER * D

    def turned(s, at):
        return (0, lax.rem(at[1] + s, SIDE))

    def fixed(s, at):
        return (0, 0)

    return pl.pallas_call(
        ssd_body,
        grid_spec=pltpu.PrefetchScalarGridSpec(
            num_scalar_prefetch=1,
            grid=(SIDE,),
            in_specs=[
                pl.BlockSpec((rows, width), turned),
                pl.BlockSpec((rows, width), turned),
                pl.BlockSpec((rows, D), turned),
                pl.BlockSpec((SSD_HEADS, rows), fixed),
                pl.BlockSpec((1, SSD_HEADS), fixed),
                pl.BlockSpec((1, width), turned),
                pl.BlockSpec((1, D, width), lambda s, at: (s, 0, 0)),
            ]
            + [pl.BlockSpec((D, width), fixed)] * SIDE,
            out_specs=pl.BlockSpec((rows, width), turned),
            scratch_shapes=[
                pltpu.VMEM((rows, SSD_HEADS), F32),
                pltpu.VMEM((8, SSD_HEADS), F32),
                pltpu.VMEM((rows, width), F32),
            ],
        ),
        out_shape=jax.ShapeDtypeStruct(gate.shape, BF),
        compiler_params=params(),
        cost_estimate=about(8),
        name="ssd_out",
    )(at, inside, gate, r, dt, rate, gain, first, *starts)


def load_queries(q_ref, qs):
    rows = q_ref.shape[0]
    for h in range(NQ):
        qs[h * rows : (h + 1) * rows, :] = q_ref[:, (2 + h) * D : (3 + h) * D]


def row_dot(a, b):
    return lax.dot_general(a, b, (((1,), (1,)), ((), ())), preferred_element_type=F32)


def lane_max(scores):
    return jnp.maximum(scores[:, :D], scores[:, D:])


def spread_max(parts):
    most = parts[0]
    for part in parts[1:]:
        most = jnp.maximum(most, part)
    return jnp.broadcast_to(jnp.max(most, axis=1, keepdims=True), most.shape)


def attention_body(at_ref, *rest):
    pieces, parts, outs = rest[:SIDE], rest[SIDE : 2 * SIDE - 1], rest[2 * SIDE - 1 : 3 * SIDE - 1]
    qs, kk, va, acc, top = rest[3 * SIDE - 1 :]
    place = pl.program_id(0)
    x, y = at_ref[0], at_ref[1]
    rows = pieces[0].shape[0]
    keys = SIDE * rows

    @pl.when(place == 0)
    def _():
        for c in range(SIDE):
            for u in range(SIDE):
                if u == 0:
                    source = pieces[c]
                else:
                    source = parts[u - 1].at[c * rows : (c + 1) * rows, :]
                to = slice(c * keys + u * rows, c * keys + (u + 1) * rows)
                kk[to, :] = source[:, :D]
                va[to, :D] = source[:, D : 2 * D]
        va[:, D:] = jnp.ones((SIDE * keys, D), BF)

    for s in range(SIDE):

        @pl.when(lax.rem(x - place + SIDE, SIDE) == s)
        def _():
            load_queries(pieces[s], qs)

    acc[...] = jnp.zeros_like(acc)
    top[...] = jnp.full_like(top, NEG)

    def chunk(c, newest):
        where = pl.ds(pl.multiple_of(lax.rem(x - c + SIDE, SIDE) * keys, keys), keys)
        kc, vc = kk.at[where, :], va.at[where, :]
        if newest:
            causal = lax.broadcasted_iota(jnp.int32, (rows, rows), 1) <= lax.broadcasted_iota(
                jnp.int32, (rows, rows), 0
            )
            shown = [0.0] + [
                jnp.where(lax.rem(y - u + SIDE, SIDE) > y, NEG, 0.0).astype(F32)
                for u in range(1, SIDE)
            ]

        def scores(h):
            mine = qs[h * 2 * rows : (h + 1) * 2 * rows, :]
            found = [row_dot(mine, kc[u * rows : (u + 1) * rows, :]) for u in range(SIDE)]
            if newest:
                found[0] = jnp.where(jnp.concatenate([causal, causal], axis=0), found[0], NEG)
            return found

        now = scores(0)
        for h in range(NQ // 2):
            following = scores(h + 1) if h + 1 < NQ // 2 else None
            mine = slice(h * 2 * rows, (h + 1) * 2 * rows)
            old = top[mine, :]
            most = [lane_max(part) for part in now]
            if newest:
                most = [part + shift for part, shift in zip(most, shown)]
            new = jnp.maximum(old, spread_max(most))
            wide = jnp.concatenate([new] * (rows // D), axis=1)
            factor = jnp.exp2((old - new) * SCALE)
            top[mine, :] = new
            out = acc[mine, :] * jnp.concatenate([factor, factor], axis=1)
            for u in range(SIDE):
                base = wide - shown[u] if newest and u else wide
                weights = jnp.exp2((now[u] - base) * SCALE).astype(BF)
                out = out + jnp.dot(
                    weights, vc[u * rows : (u + 1) * rows, :], preferred_element_type=F32
                )
            acc[mine, :] = out
            now = following

    def older(c, carry):
        chunk(c, False)
        return carry

    lax.fori_loop(0, place, older, 0)
    chunk(place, True)
    for s in range(SIDE):

        @pl.when(lax.rem(x - place + SIDE, SIDE) == s)
        def _():
            for h in range(NQ):
                mine = slice(h * rows, (h + 1) * rows)
                outs[s][:, h * D : (h + 1) * D] = (acc[mine, :D] / acc[mine, D:]).astype(BF)


def attention(at, pieces, parts):
    rows, width = pieces[0].shape
    given = width - 2 * D
    keys = parts[0].shape[0]

    def fixed(place, at):
        return (0, 0)

    return pl.pallas_call(
        attention_body,
        grid_spec=pltpu.PrefetchScalarGridSpec(
            num_scalar_prefetch=1,
            grid=(SIDE,),
            in_specs=[pl.BlockSpec((rows, width), fixed)] * SIDE
            + [pl.BlockSpec((keys, 2 * D), fixed)] * (SIDE - 1),
            out_specs=[pl.BlockSpec((rows, given), fixed)] * SIDE,
            scratch_shapes=[
                pltpu.VMEM((NQ * rows, D), BF),
                pltpu.VMEM((SIDE * keys, D), BF),
                pltpu.VMEM((SIDE * keys, 2 * D), BF),
                pltpu.VMEM((NQ * rows, 2 * D), F32),
                pltpu.VMEM((NQ * rows, D), F32),
            ],
        ),
        out_shape=[jax.ShapeDtypeStruct((rows, given), BF)] * SIDE,
        compiler_params=params(28),
        cost_estimate=about(18),
        name="attention",
    )(at, *pieces, *parts)


def unpack_body(at_ref, *refs):
    ins, out = refs[:SIDE], refs[SIDE]
    width = ins[0].shape[1]
    for s in range(SIDE):
        out[:, columns(lax.rem(at_ref[0] + s, SIDE), width)] = ins[s][...]


def unpack(at, pieces):
    rows, width = pieces[0].shape
    return pl.pallas_call(
        unpack_body,
        in_specs=[pl.BlockSpec(memory_space=pltpu.SMEM)]
        + [pl.BlockSpec(memory_space=pltpu.VMEM)] * SIDE,
        out_specs=pl.BlockSpec(memory_space=pltpu.VMEM),
        out_shape=jax.ShapeDtypeStruct((rows, SIDE * width), BF),
        compiler_params=params(),
        cost_estimate=about(2),
        name="unpack",
    )(at, *pieces)


def shifted(value, axis, by):
    return lax.ppermute(value, axis, [(i, (i + by) % SIDE) for i in range(SIDE)])


def exchange(pieces, axis, sign):
    return [pieces[0]] + [shifted(pieces[s], axis, sign * s) for s in range(1, SIDE)]


def local(
    ssd_input, gate_input, write_map, read_map, step_size, decay_log, skip_gain, norm_gain,
    query_rows, key_rows, value_rows,
):
    step_size = step_size.T
    at = jnp.stack([lax.axis_index("x"), lax.axis_index("y")]).astype(jnp.int32)
    rate = decay_log.reshape(1, -1)
    skip = skip_gain.reshape(1, -1)
    gain = norm_gain.reshape(1, -1)
    tie = lax.optimization_barrier
    *states, first = local_states(at, ssd_input, write_map, step_size, rate)
    states, packed = tie((states, (key_rows, value_rows, query_rows)))
    states = exchange(states, "y", 1)
    pieces = exchange(pack(at, *packed), "x", 1)
    inside = inside_spans(at, ssd_input, write_map, read_map, step_size, rate, skip)
    pieces, inside = tie((pieces, inside))
    own = stack(pieces)
    middle = own.shape[0] // 2
    before = shifted(own, "y", 1)
    after = shifted(own, "y", -1)
    states, inside = tie((states, inside))
    totals = exchange(row_total(at, states), "x", 1)
    entering = entering_rows(at, totals)
    entering, before, after = tie((entering, before, after))
    far = [shifted(before[:middle], "y", 1), shifted(after[middle:], "y", -1)]
    entering = exchange(entering, "x", -1)
    starts = start_states(at, states, entering)
    starts, pieces = tie((starts, pieces))
    starts = exchange(starts, "y", -1)
    parts = [before, jnp.concatenate(far, axis=0), after]
    back = exchange(attention(at, pieces, parts), "x", -1)
    ssd = ssd_out_of(at, inside, gate_input, read_map, step_size, rate, gain, first, starts)
    ssd, back = tie((ssd, back))
    return (ssd, unpack(at, back))


def solution(mesh):
    grid = Mesh(mesh.devices.reshape(-1, SIDE, SIDE), ("dp", "x", "y"))
    split = P(("dp", "x", "y"), None)
    in_specs = (split,) * 5 + (P(), P(), P()) + (split,) * 3
    return jax.shard_map(
        local, mesh=grid, in_specs=in_specs, out_specs=(split, split), check_vma=False
    )
```

```python
import math

import jax
import jax.numpy as jnp
from jax import lax
from jax.experimental import pallas as pl
from jax.experimental.pallas import tpu as pltpu
from jax.sharding import Mesh, PartitionSpec as P

SSD_HEADS = 32
GROUPS = 4
PER = SSD_HEADS // GROUPS
D = 128
NQ = 4
KV_HEADS = 4
SIDE = 4
SCALE = (D**-0.5) * math.log2(math.e)
LOG2E = math.log2(math.e)
BF = jnp.bfloat16
F32 = jnp.float32
NEG = -1e30
EXTRA = 8


def params(mib=16):
    return pltpu.CompilerParams(vmem_limit_bytes=mib << 20)


def about(us):
    return pl.CostEstimate(
        flops=int(us * 1.0e9), bytes_accessed=int(us * 3.0e6), transcendentals=0
    )


def columns(begin, width):
    return pl.ds(pl.multiple_of(begin * width, D), width)


def pack_body(at_ref, *refs):
    outs = refs[3 * SIDE :]
    for s in range(SIDE):
        outs[s][:, :D] = refs[3 * s][...]
        outs[s][:, D : 2 * D] = refs[3 * s + 1][...]
        outs[s][:, 2 * D :] = refs[3 * s + 2][...]


def pack(at, k, v, q):
    rows, cols = q.shape
    width = cols // SIDE

    def spec(s, width):
        return pl.BlockSpec((rows, width), lambda g, at: (0, lax.rem(at[0] + s, SIDE)))

    return pl.pallas_call(
        pack_body,
        grid_spec=pltpu.PrefetchScalarGridSpec(
            num_scalar_prefetch=1,
            grid=(1,),
            in_specs=[spec(s, w) for s in range(SIDE) for w in (D, D, width)],
            out_specs=[pl.BlockSpec((rows, 2 * D + width), lambda g, at: (0, 0))] * SIDE,
        ),
        out_shape=[jax.ShapeDtypeStruct((rows, 2 * D + width), BF)] * SIDE,
        compiler_params=params(),
        name="pack",
    )(at, *([k, v, q] * SIDE))


def stack_body(*refs):
    ins, out = refs[:SIDE], refs[SIDE]
    rows = ins[0].shape[0]
    for s in range(SIDE):
        out[s * rows : (s + 1) * rows, :] = ins[s][...]


def stack(pieces):
    rows = pieces[0].shape[0]
    return pl.pallas_call(
        stack_body,
        grid=(1,),
        in_specs=[pl.BlockSpec((rows, 2 * D), lambda g: (0, 0))] * SIDE,
        out_specs=pl.BlockSpec((SIDE * rows, 2 * D), lambda g: (0, 0)),
        out_shape=jax.ShapeDtypeStruct((SIDE * rows, 2 * D), BF),
        compiler_params=params(),
        name="stack",
    )(*pieces)


def span_sums(log_decay, span):
    row = lax.rem(lax.broadcasted_iota(jnp.int32, log_decay.shape, 0), span)
    step = 1
    while step < span:
        moved = pltpu.roll(log_decay, step, 0)
        log_decay = log_decay + jnp.where(row >= step, moved, 0.0)
        step *= 2
    return log_decay


def state_body(at_ref, x_hbm, w_hbm, dt_hbm, rate_hbm, *rest):
    outs, first_ref, (x_ref, w_ref, dt_ref, rate_ref, sems) = rest[:SIDE], rest[SIDE], rest[SIDE + 1 :]
    rows = dt_ref.shape[1]
    half = rows // 2
    width = PER * D
    y = at_ref[1]
    steps = pltpu.make_async_copy(dt_hbm, dt_ref, sems.at[2 * SIDE])
    steps.start()
    rates = pltpu.make_async_copy(rate_hbm, rate_ref, sems.at[2 * SIDE + 1])
    rates.start()
    arrivals = []
    for s in (1, 3, 2, 0):
        group = lax.rem(y + s, SIDE)
        arrivals.append(
            (
                s,
                pltpu.make_async_copy(
                    w_hbm.at[:, columns(group, D)], w_ref.at[s], sems.at[SIDE + s]
                ),
                pltpu.make_async_copy(
                    x_hbm.at[:, columns(group, width)], x_ref.at[s], sems.at[s]
                ),
            )
        )
    for _, w_copy, x_copy in arrivals:
        w_copy.start()
        x_copy.start()
    steps.wait()
    rates.wait()
    dt = jnp.transpose(dt_ref[...])
    sums = span_sums(dt * (-jnp.exp(rate_ref[...])), half)
    ends = jnp.concatenate(
        [jnp.broadcast_to(sums[half * c + half - 1 : half * c + half], (half, SSD_HEADS)) for c in range(2)],
        axis=0,
    )
    to_end = jnp.exp(ends - sums) * dt
    last = ends[half : half + 8]
    total = ends[:8] + last
    for s, w_copy, x_copy in arrivals:
        turn = SSD_HEADS - PER * lax.rem(y + s, SIDE)
        mine, last_mine, total_mine = [
            pltpu.roll(jnp.concatenate([part] * (D // SSD_HEADS), axis=1), turn, 1)
            for part in (to_end, last, total)
        ]
        w_copy.wait()
        x_copy.wait()
        scaled = jnp.concatenate(
            [
                (mine[:, j : j + 1] * x_ref[s, :, j * D : (j + 1) * D].astype(F32)).astype(BF)
                for j in range(PER)
            ],
            axis=1,
        )
        first, second = [
            lax.dot_general(
                w_ref[s, c * half : (c + 1) * half, :],
                scaled[c * half : (c + 1) * half],
                (((0,), (0,)), ((), ())),
                preferred_element_type=F32,
            )
            for c in range(2)
        ]
        first_ref[s] = first
        decay = jnp.concatenate(
            [jnp.broadcast_to(last_mine[0:1, j : j + 1], (1, D)) for j in range(PER)], axis=1
        )
        outs[s][:D, :] = jnp.exp(decay) * first + second
        outs[s][D:, :] = jnp.concatenate(
            [jnp.broadcast_to(total_mine[:, j : j + 1], (EXTRA, D)) for j in range(PER)], axis=1
        )


def local_states(at, x, w, dt, rate):
    rows = x.shape[0]
    width = PER * D
    far = pl.BlockSpec(memory_space=pltpu.HBM)
    near = pl.BlockSpec(memory_space=pltpu.VMEM)
    return pl.pallas_call(
        state_body,
        in_specs=[pl.BlockSpec(memory_space=pltpu.SMEM), far, far, far, far],
        out_specs=[near] * (SIDE + 1),
        scratch_shapes=[
            pltpu.VMEM((SIDE, rows, width), BF),
            pltpu.VMEM((SIDE, rows, D), BF),
            pltpu.VMEM((SSD_HEADS, rows), F32),
            pltpu.VMEM((1, SSD_HEADS), F32),
            pltpu.SemaphoreType.DMA((2 * SIDE + 2,)),
        ],
        out_shape=[jax.ShapeDtypeStruct((D + EXTRA, width), F32)] * SIDE
        + [jax.ShapeDtypeStruct((SIDE, D, width), F32)],
        compiler_params=params(),
        name="local_states",
    )(at, *[pltpu.with_memory_space_constraint(part, pltpu.HBM) for part in (x, w, dt, rate)])


def flag(condition):
    return jnp.where(condition, 1.0, 0.0).astype(F32)


def row_total_body(at_ref, *refs):
    ins, outs, total = refs[:SIDE], refs[SIDE : 2 * SIDE], refs[2 * SIDE]
    x, y = at_ref[0], at_ref[1]
    place = [lax.rem(y - s + SIDE, SIDE) for s in range(SIDE)]
    logs = [ref[D : D + 1, :] for ref in ins]
    value = None
    for s in range(SIDE):
        later = sum(flag(place[u] > place[s]) * logs[u] for u in range(SIDE) if u != s)
        term = ins[s][:D, :] * jnp.exp(later)
        value = term if value is None else value + term
    total[:D, :] = value
    total[D:, :] = jnp.broadcast_to(logs[0] + logs[1] + logs[2] + logs[3], (EXTRA, value.shape[1]))
    width = value.shape[1] // SIDE
    for s in range(SIDE):
        begin = pl.multiple_of(lax.rem(x + s, SIDE) * width, width)
        outs[s][...] = total[:, pl.ds(begin, width)]


def row_total(at, states):
    rows, width = states[0].shape
    return pl.pallas_call(
        row_total_body,
        in_specs=[pl.BlockSpec(memory_space=pltpu.SMEM)] + [pl.BlockSpec(memory_space=pltpu.VMEM)] * SIDE,
        out_specs=[pl.BlockSpec(memory_space=pltpu.VMEM)] * SIDE,
        out_shape=[jax.ShapeDtypeStruct((rows, width // SIDE), F32)] * SIDE,
        scratch_shapes=[pltpu.VMEM((rows, width), F32)],
        compiler_params=params(),
        cost_estimate=about(2),
        name="row_total",
    )(at, *states)


def entering_body(at_ref, *refs):
    ins, outs = refs[:SIDE], refs[SIDE:]
    prefixes(at_ref[0], ins, outs, None)


def prefixes(mine, ins, outs, entering):
    place = [lax.rem(mine - s + SIDE, SIDE) for s in range(SIDE)]
    logs = [ref[D : D + 1, :] for ref in ins]
    for t in range(SIDE):
        if entering is None:
            state = jnp.zeros((D, ins[0].shape[1]), F32)
        else:
            before = sum(flag(place[u] < place[t]) * logs[u] for u in range(SIDE) if u != t)
            state = jnp.exp(before) * entering
        for s in range(SIDE):
            if s == t:
                continue
            gap = sum(
                flag((place[u] > place[s]) & (place[u] < place[t])) * logs[u]
                for u in range(SIDE)
                if u != t and u != s
            )
            state = state + (flag(place[s] < place[t]) * jnp.exp(gap)) * ins[s][:D, :]
        outs[t][...] = state


def entering_rows(at, totals):
    width = totals[0].shape[1]
    return pl.pallas_call(
        entering_body,
        in_specs=[pl.BlockSpec(memory_space=pltpu.SMEM)] + [pl.BlockSpec(memory_space=pltpu.VMEM)] * SIDE,
        out_specs=[pl.BlockSpec(memory_space=pltpu.VMEM)] * SIDE,
        out_shape=[jax.ShapeDtypeStruct((D, width), F32)] * SIDE,
        compiler_params=params(),
        cost_estimate=about(1),
        name="entering_rows",
    )(at, *totals)


def starts_body(at_ref, *refs):
    ins, pieces = refs[:SIDE], refs[SIDE : 2 * SIDE]
    outs, whole = refs[2 * SIDE : 3 * SIDE], refs[3 * SIDE]
    width = pieces[0].shape[1]
    for s in range(SIDE):
        begin = pl.multiple_of(lax.rem(at_ref[0] + s, SIDE) * width, width)
        whole[:, pl.ds(begin, width)] = pieces[s][...]
    prefixes(at_ref[1], ins, outs, whole[...])


def start_states(at, states, entering):
    width = states[0].shape[1]
    return pl.pallas_call(
        starts_body,
        in_specs=[pl.BlockSpec(memory_space=pltpu.SMEM)]
        + [pl.BlockSpec(memory_space=pltpu.VMEM)] * (2 * SIDE),
        out_specs=[pl.BlockSpec(memory_space=pltpu.VMEM)] * SIDE,
        out_shape=[jax.ShapeDtypeStruct((D, width), F32)] * SIDE,
        scratch_shapes=[pltpu.VMEM((D, width), F32)],
        compiler_params=params(),
        cost_estimate=about(2),
        name="start_states",
    )(at, *states, *entering)


def inside_body(at_ref, x_ref, w_ref, r_ref, dt_ref, rate_ref, skip_ref, out_ref, cum, cum_t):
    s = pl.program_id(0)
    rows = dt_ref.shape[1]
    half = rows // 2
    group = lax.rem(at_ref[1] + s, SIDE)

    @pl.when(s == 0)
    def _():
        dt = jnp.transpose(dt_ref[...])
        sums = span_sums(dt * (-jnp.exp(rate_ref[...])), half)
        cum[...] = sums * LOG2E
        cum_t[...] = jnp.transpose((sums - jnp.log(dt)) * LOG2E)

    row = lax.broadcasted_iota(jnp.int32, (half, half), 0)
    col = lax.broadcasted_iota(jnp.int32, (half, half), 1)
    causal = col <= row
    spans = [slice(c * half, (c + 1) * half) for c in range(2)]
    pairs = [row_dot(r_ref[span, :], w_ref[span, :]) for span in spans]

    for g in range(GROUPS):

        @pl.when(group == g)
        def _():
            for j in range(PER):
                h = g * PER + j
                lanes = slice(j * D, (j + 1) * D)
                for c, span in enumerate(spans):
                    x = x_ref[span, lanes]
                    down = jnp.broadcast_to(cum[span, h : h + 1], (half, half))
                    weights = pairs[c] * jnp.exp2(down - cum_t[h : h + 1, span])
                    weights = jnp.where(causal, weights, 0.0).astype(BF)
                    out_ref[span, lanes] = jnp.dot(
                        weights, x, preferred_element_type=F32
                    ) + skip_ref[0, h] * x.astype(F32)


def inside_spans(at, x, w, r, dt, rate, skip):
    rows = x.shape[0]
    width = PER * D

    def turned(s, at):
        return (0, lax.rem(at[1] + s, SIDE))

    def fixed(s, at):
        return (0, 0)

    return pl.pallas_call(
        inside_body,
        grid_spec=pltpu.PrefetchScalarGridSpec(
            num_scalar_prefetch=1,
            grid=(SIDE,),
            in_specs=[
                pl.BlockSpec((rows, width), turned),
                pl.BlockSpec((rows, D), turned),
                pl.BlockSpec((rows, D), turned),
                pl.BlockSpec((SSD_HEADS, rows), fixed),
                pl.BlockSpec((1, SSD_HEADS), fixed),
                pl.BlockSpec(memory_space=pltpu.SMEM),
            ],
            out_specs=pl.BlockSpec((rows, width), turned),
            scratch_shapes=[
                pltpu.VMEM((rows, SSD_HEADS), F32),
                pltpu.VMEM((SSD_HEADS, rows), F32),
            ],
        ),
        out_shape=jax.ShapeDtypeStruct(x.shape, F32),
        compiler_params=params(),
        name="inside_spans",
    )(at, x, w, r, dt, rate, skip)


def ssd_body(
    at_ref, inside_ref, gate_ref, r_ref, dt_ref, rate_ref, gain_ref, first_ref, *rest
):
    starts, out_hbm, (gated, staged, sems) = rest[:SIDE], rest[SIDE], rest[SIDE + 1 :]
    y = at_ref[1]
    rows = dt_ref.shape[1]
    half = rows // 2
    width = PER * D
    sums = span_sums(jnp.transpose(dt_ref[...]) * (-jnp.exp(rate_ref[...])), half)
    ends = jnp.broadcast_to(sums[half - 1 : half], (8, SSD_HEADS))
    copies = []
    for s in (0, 1, 3, 2):
        group = lax.rem(y + s, SIDE)
        turn = SSD_HEADS - PER * group
        grown, decay = [
            jnp.exp(pltpu.roll(jnp.concatenate([part] * (D // SSD_HEADS), axis=1), turn, 1))
            for part in (sums, ends)
        ]
        decay = jnp.concatenate(
            [jnp.broadcast_to(decay[0:1, j : j + 1], (1, D)) for j in range(PER)], axis=1
        )
        read = r_ref[:, columns(group, D)]
        start = starts[s][...]
        gated[:half, :] = jnp.dot(read[:half], start.astype(BF), preferred_element_type=F32)
        gated[half:, :] = jnp.dot(
            read[half:], (decay * start + first_ref[s]).astype(BF), preferred_element_type=F32
        )
        square = jnp.zeros((rows, D), F32)
        for j in range(PER):
            lanes = slice(j * D, (j + 1) * D)
            there = columns(group * PER + j, D)
            mixed = inside_ref[:, there] + grown[:, j : j + 1] * gated[:, lanes]
            gate = gate_ref[:, there].astype(F32)
            value = mixed * (gate * (0.5 + 0.5 * jnp.tanh(0.5 * gate)))
            gated[:, lanes] = value
            square = square + value * value
        mean = jnp.sum(square, axis=1, keepdims=True) * (1.0 / width)
        inverse = lax.rsqrt(mean + 1e-05)
        for j in range(PER):
            lanes = slice(j * D, (j + 1) * D)
            there = columns(group * PER + j, D)
            staged[s, :, lanes] = (
                gated[:, lanes] * inverse * gain_ref[:, there].astype(F32)
            ).astype(BF)
        copy = pltpu.make_async_copy(
            staged.at[s], out_hbm.at[:, columns(group, width)], sems.at[s]
        )
        copy.start()
        copies.append(copy)
    for copy in copies:
        copy.wait()


def ssd_out_of(at, inside, gate, r, dt, rate, gain, first, starts):
    rows = inside.shape[0]
    width = PER * D
    near = pl.BlockSpec(memory_space=pltpu.VMEM)
    return pl.pallas_call(
        ssd_body,
        in_specs=[pl.BlockSpec(memory_space=pltpu.SMEM)] + [near] * (7 + SIDE),
        out_specs=pl.BlockSpec(memory_space=pltpu.HBM),
        scratch_shapes=[
            pltpu.VMEM((rows, width), F32),
            pltpu.VMEM((SIDE, rows, width), BF),
            pltpu.SemaphoreType.DMA((SIDE,)),
        ],
        out_shape=jax.ShapeDtypeStruct(gate.shape, BF),
        compiler_params=params(24),
        cost_estimate=about(8),
        name="ssd_out",
    )(at, inside, gate, r, dt, rate, gain, first, *starts)


def load_queries(q_ref, qs):
    rows = q_ref.shape[0]
    for h in range(NQ):
        qs[h * rows : (h + 1) * rows, :] = q_ref[:, (2 + h) * D : (3 + h) * D]


def row_dot(a, b):
    return lax.dot_general(a, b, (((1,), (1,)), ((), ())), preferred_element_type=F32)


def lane_max(scores):
    return jnp.maximum(scores[:, :D], scores[:, D:])


def spread_max(parts):
    most = parts[0]
    for part in parts[1:]:
        most = jnp.maximum(most, part)
    return jnp.broadcast_to(jnp.max(most, axis=1, keepdims=True), most.shape)


def attention_body(at_ref, *rest):
    pieces, parts, outs = rest[:SIDE], rest[SIDE : 2 * SIDE], rest[2 * SIDE : 3 * SIDE]
    qs, acc, top = rest[3 * SIDE :]
    place = pl.program_id(0)
    x, y = at_ref[0], at_ref[1]
    rows = pieces[0].shape[0]
    ones = jnp.ones((rows, D), BF)

    for s in range(SIDE):

        @pl.when(lax.rem(x - place + SIDE, SIDE) == s)
        def _():
            load_queries(pieces[s], qs)

    acc[...] = jnp.zeros_like(acc)
    top[...] = jnp.full_like(top, NEG)

    def chunk(c, newest):
        where = pl.ds(pl.multiple_of(lax.rem(x - c + SIDE, SIDE) * rows, rows), rows)
        if newest:
            causal = lax.broadcasted_iota(jnp.int32, (rows, rows), 1) <= lax.broadcasted_iota(
                jnp.int32, (rows, rows), 0
            )
            shown = [0.0] + [
                jnp.where(lax.rem(y - u + SIDE, SIDE) > y, NEG, 0.0).astype(F32)
                for u in range(1, SIDE)
            ]

        def scores(h):
            mine = qs[h * 2 * rows : (h + 1) * 2 * rows, :]
            found = [row_dot(mine, part[where, :D]) for part in parts]
            if newest:
                found[0] = jnp.where(jnp.concatenate([causal, causal], axis=0), found[0], NEG)
            return found

        now = scores(0)
        for h in range(NQ // 2):
            following = scores(h + 1) if h + 1 < NQ // 2 else None
            mine = slice(h * 2 * rows, (h + 1) * 2 * rows)
            old = top[mine, :]
            most = [lane_max(part) for part in now]
            if newest:
                most = [part + shift for part, shift in zip(most, shown)]
            new = jnp.maximum(old, spread_max(most))
            wide = jnp.concatenate([new] * (rows // D), axis=1)
            factor = jnp.exp2((old - new) * SCALE)
            top[mine, :] = new
            out = acc[mine, :] * jnp.concatenate([factor, factor], axis=1)
            for u in range(SIDE):
                base = wide - shown[u] if newest and u else wide
                weights = jnp.exp2((now[u] - base) * SCALE).astype(BF)
                values = jnp.concatenate([parts[u][where, D:], ones], axis=1)
                out = out + jnp.dot(weights, values, preferred_element_type=F32)
            acc[mine, :] = out
            now = following

    def older(c, carry):
        chunk(c, False)
        return carry

    lax.fori_loop(0, place, older, 0)
    chunk(place, True)
    for s in range(SIDE):

        @pl.when(lax.rem(x - place + SIDE, SIDE) == s)
        def _():
            for h in range(NQ):
                mine = slice(h * rows, (h + 1) * rows)
                outs[s][:, h * D : (h + 1) * D] = (acc[mine, :D] / acc[mine, D:]).astype(BF)


def attention(at, pieces, parts):
    rows, width = pieces[0].shape
    given = width - 2 * D

    near = pl.BlockSpec(memory_space=pltpu.VMEM)

    return pl.pallas_call(
        attention_body,
        grid_spec=pltpu.PrefetchScalarGridSpec(
            num_scalar_prefetch=1,
            grid=(SIDE,),
            in_specs=[near] * (2 * SIDE),
            out_specs=[near] * SIDE,
            scratch_shapes=[
                pltpu.VMEM((NQ * rows, D), BF),
                pltpu.VMEM((NQ * rows, 2 * D), F32),
                pltpu.VMEM((NQ * rows, D), F32),
            ],
        ),
        out_shape=[jax.ShapeDtypeStruct((rows, given), BF)] * SIDE,
        compiler_params=params(28),
        cost_estimate=about(18),
        name="attention",
    )(at, *pieces, *parts)


def unpack_body(at_ref, *refs):
    ins, out, sems = refs[:SIDE], refs[SIDE], refs[SIDE + 1]
    width = ins[0].shape[1]
    copies = [
        pltpu.make_async_copy(
            ins[s], out.at[:, columns(lax.rem(at_ref[0] + s, SIDE), width)], sems.at[s]
        )
        for s in range(SIDE)
    ]
    for copy in copies:
        copy.start()
    for copy in copies:
        copy.wait()


def unpack(at, pieces):
    rows, width = pieces[0].shape
    return pl.pallas_call(
        unpack_body,
        in_specs=[pl.BlockSpec(memory_space=pltpu.SMEM)]
        + [pl.BlockSpec(memory_space=pltpu.VMEM)] * SIDE,
        out_specs=pl.BlockSpec(memory_space=pltpu.HBM),
        out_shape=jax.ShapeDtypeStruct((rows, SIDE * width), BF),
        scratch_shapes=[pltpu.SemaphoreType.DMA((SIDE,))],
        compiler_params=params(),
        cost_estimate=about(2),
        name="unpack",
    )(at, *pieces)


def shifted(value, axis, by):
    return lax.ppermute(value, axis, [(i, (i + by) % SIDE) for i in range(SIDE)])


def exchange(pieces, axis, sign):
    return [pieces[0]] + [shifted(pieces[s], axis, sign * s) for s in range(1, SIDE)]


def local(
    ssd_input, gate_input, write_map, read_map, step_size, decay_log, skip_gain, norm_gain,
    query_rows, key_rows, value_rows,
):
    step_size = step_size.T
    at = jnp.stack([lax.axis_index("x"), lax.axis_index("y")]).astype(jnp.int32)
    rate = decay_log.reshape(1, -1)
    skip = skip_gain.reshape(1, -1)
    gain = norm_gain.reshape(1, -1)
    tie = lax.optimization_barrier
    *states, first = local_states(at, ssd_input, write_map, step_size, rate)
    states, packed = tie((states, (key_rows, value_rows, query_rows)))
    states = exchange(states, "y", 1)
    pieces = exchange(pack(at, *packed), "x", 1)
    inside = inside_spans(at, ssd_input, write_map, read_map, step_size, rate, skip)
    pieces, inside = tie((pieces, inside))
    own = stack(pieces)
    middle = own.shape[0] // 2
    before = shifted(own, "y", 1)
    after = shifted(own, "y", -1)
    states, inside = tie((states, inside))
    totals = exchange(row_total(at, states), "x", 1)
    entering = entering_rows(at, totals)
    entering, before, after = tie((entering, before, after))
    far = [shifted(before[:middle], "y", 1), shifted(after[middle:], "y", -1)]
    entering = exchange(entering, "x", -1)
    starts = start_states(at, states, entering)
    starts, pieces = tie((starts, pieces))
    starts = exchange(starts, "y", -1)
    parts = [own, before, jnp.concatenate(far, axis=0), after]
    back = exchange(attention(at, pieces, parts), "x", -1)
    ssd = ssd_out_of(at, inside, gate_input, read_map, step_size, rate, gain, first, starts)
    ssd, back = tie((ssd, back))
    return (ssd, unpack(at, back))


def solution(mesh):
    grid = Mesh(mesh.devices.reshape(-1, SIDE, SIDE), ("dp", "x", "y"))
    split = P(("dp", "x", "y"), None)
    in_specs = (split,) * 5 + (P(), P(), P()) + (split,) * 3
    return jax.shard_map(
        local, mesh=grid, in_specs=in_specs, out_specs=(split, split), check_vma=False
    )
```

```python
import functools
import math

import jax
import jax.numpy as jnp
from jax import lax
from jax.experimental import pallas as pl
from jax.experimental.pallas import tpu as pltpu
from jax.sharding import Mesh, PartitionSpec as P

SSD_HEADS = 32
GROUPS = 4
PER = SSD_HEADS // GROUPS
D = 128
NQ = 4
KV_HEADS = 4
SIDE = 4
SCALE = (D**-0.5) * math.log2(math.e)
LOG2E = math.log2(math.e)
BF = jnp.bfloat16
F32 = jnp.float32
NEG = -1e30
EXTRA = 8


def params(mib=16):
    return pltpu.CompilerParams(vmem_limit_bytes=mib << 20)


def about(us):
    return pl.CostEstimate(
        flops=int(us * 1.0e9), bytes_accessed=int(us * 3.0e6), transcendentals=0
    )


def columns(begin, width):
    return pl.ds(pl.multiple_of(begin * width, D), width)


def pack_body(at_ref, *refs):
    outs = refs[3 * SIDE :]
    for s in range(SIDE):
        outs[s][:, :D] = refs[3 * s][...]
        outs[s][:, D : 2 * D] = refs[3 * s + 1][...]
        outs[s][:, 2 * D :] = refs[3 * s + 2][...]


def pack(at, k, v, q):
    rows, cols = q.shape
    width = cols // SIDE

    def spec(s, width):
        return pl.BlockSpec((rows, width), lambda g, at: (0, lax.rem(at[0] + s, SIDE)))

    return pl.pallas_call(
        pack_body,
        grid_spec=pltpu.PrefetchScalarGridSpec(
            num_scalar_prefetch=1,
            grid=(1,),
            in_specs=[spec(s, w) for s in range(SIDE) for w in (D, D, width)],
            out_specs=[pl.BlockSpec((rows, 2 * D + width), lambda g, at: (0, 0))] * SIDE,
        ),
        out_shape=[jax.ShapeDtypeStruct((rows, 2 * D + width), BF)] * SIDE,
        compiler_params=params(),
        name="pack",
    )(at, *([k, v, q] * SIDE))


def stack_body(*refs):
    ins, out = refs[:SIDE], refs[SIDE]
    rows = ins[0].shape[0]
    for s in range(SIDE):
        out[s * rows : (s + 1) * rows, :] = ins[s][...]


def stack(pieces):
    rows = pieces[0].shape[0]
    return pl.pallas_call(
        stack_body,
        grid=(1,),
        in_specs=[pl.BlockSpec((rows, 2 * D), lambda g: (0, 0))] * SIDE,
        out_specs=pl.BlockSpec((SIDE * rows, 2 * D), lambda g: (0, 0)),
        out_shape=jax.ShapeDtypeStruct((SIDE * rows, 2 * D), BF),
        compiler_params=params(),
        name="stack",
    )(*pieces)


def span_sums(log_decay, span):
    row = lax.rem(lax.broadcasted_iota(jnp.int32, log_decay.shape, 0), span)
    step = 1
    while step < span:
        moved = pltpu.roll(log_decay, step, 0)
        log_decay = log_decay + jnp.where(row >= step, moved, 0.0)
        step *= 2
    return log_decay


def state_body(slots, at_ref, x_hbm, w_hbm, dt_hbm, rate_hbm, *rest):
    n = len(slots)
    outs, first_ref, (x_ref, w_ref, dt_ref, rate_ref, sems) = rest[:n], rest[n], rest[n + 1 :]
    rows = dt_ref.shape[1]
    half = rows // 2
    width = PER * D
    y = at_ref[1]
    steps = pltpu.make_async_copy(dt_hbm, dt_ref, sems.at[2 * n])
    steps.start()
    rates = pltpu.make_async_copy(rate_hbm, rate_ref, sems.at[2 * n + 1])
    rates.start()
    arrivals = []
    for i, s in enumerate(slots):
        group = lax.rem(y + s, SIDE)
        arrivals.append(
            (
                i,
                s,
                pltpu.make_async_copy(
                    w_hbm.at[:, columns(group, D)], w_ref.at[i], sems.at[n + i]
                ),
                pltpu.make_async_copy(
                    x_hbm.at[:, columns(group, width)], x_ref.at[i], sems.at[i]
                ),
            )
        )
    for _, _, w_copy, x_copy in arrivals:
        w_copy.start()
        x_copy.start()
    steps.wait()
    rates.wait()
    dt = jnp.transpose(dt_ref[...])
    sums = span_sums(dt * (-jnp.exp(rate_ref[...])), half)
    ends = jnp.concatenate(
        [jnp.broadcast_to(sums[half * c + half - 1 : half * c + half], (half, SSD_HEADS)) for c in range(2)],
        axis=0,
    )
    to_end = jnp.exp(ends - sums) * dt
    last = ends[half : half + 8]
    total = ends[:8] + last
    for i, s, w_copy, x_copy in arrivals:
        turn = SSD_HEADS - PER * lax.rem(y + s, SIDE)
        mine, last_mine, total_mine = [
            pltpu.roll(jnp.concatenate([part] * (D // SSD_HEADS), axis=1), turn, 1)
            for part in (to_end, last, total)
        ]
        w_copy.wait()
        x_copy.wait()
        scaled = jnp.concatenate(
            [
                (mine[:, j : j + 1] * x_ref[i, :, j * D : (j + 1) * D].astype(F32)).astype(BF)
                for j in range(PER)
            ],
            axis=1,
        )
        first, second = [
            lax.dot_general(
                w_ref[i, c * half : (c + 1) * half, :],
                scaled[c * half : (c + 1) * half],
                (((0,), (0,)), ((), ())),
                preferred_element_type=F32,
            )
            for c in range(2)
        ]
        first_ref[i] = first
        decay = jnp.concatenate(
            [jnp.broadcast_to(last_mine[0:1, j : j + 1], (1, D)) for j in range(PER)], axis=1
        )
        outs[i][:D, :] = jnp.exp(decay) * first + second
        outs[i][D:, :] = jnp.concatenate(
            [jnp.broadcast_to(total_mine[:, j : j + 1], (EXTRA, D)) for j in range(PER)], axis=1
        )


def local_states(at, slots, x, w, dt, rate):
    n = len(slots)
    rows = x.shape[0]
    width = PER * D
    far = pl.BlockSpec(memory_space=pltpu.HBM)
    near = pl.BlockSpec(memory_space=pltpu.VMEM)
    return pl.pallas_call(
        functools.partial(state_body, slots),
        in_specs=[pl.BlockSpec(memory_space=pltpu.SMEM), far, far, far, far],
        out_specs=[near] * (n + 1),
        scratch_shapes=[
            pltpu.VMEM((n, rows, width), BF),
            pltpu.VMEM((n, rows, D), BF),
            pltpu.VMEM((SSD_HEADS, rows), F32),
            pltpu.VMEM((1, SSD_HEADS), F32),
            pltpu.SemaphoreType.DMA((2 * n + 2,)),
        ],
        out_shape=[jax.ShapeDtypeStruct((D + EXTRA, width), F32)] * n
        + [jax.ShapeDtypeStruct((n, D, width), F32)],
        compiler_params=params(),
        name="local_states",
    )(at, *[pltpu.with_memory_space_constraint(part, pltpu.HBM) for part in (x, w, dt, rate)])


def flag(condition):
    return jnp.where(condition, 1.0, 0.0).astype(F32)


def row_total_body(at_ref, *refs):
    ins, outs, total = refs[:SIDE], refs[SIDE : 2 * SIDE], refs[2 * SIDE]
    x, y = at_ref[0], at_ref[1]
    place = [lax.rem(y - s + SIDE, SIDE) for s in range(SIDE)]
    logs = [ref[D : D + 1, :] for ref in ins]
    value = None
    for s in range(SIDE):
        later = sum(flag(place[u] > place[s]) * logs[u] for u in range(SIDE) if u != s)
        term = ins[s][:D, :] * jnp.exp(later)
        value = term if value is None else value + term
    total[:D, :] = value
    total[D:, :] = jnp.broadcast_to(logs[0] + logs[1] + logs[2] + logs[3], (EXTRA, value.shape[1]))
    width = value.shape[1] // SIDE
    for s in range(SIDE):
        begin = pl.multiple_of(lax.rem(x + s, SIDE) * width, width)
        outs[s][...] = total[:, pl.ds(begin, width)]


def row_total(at, states):
    rows, width = states[0].shape
    return pl.pallas_call(
        row_total_body,
        in_specs=[pl.BlockSpec(memory_space=pltpu.SMEM)] + [pl.BlockSpec(memory_space=pltpu.VMEM)] * SIDE,
        out_specs=[pl.BlockSpec(memory_space=pltpu.VMEM)] * SIDE,
        out_shape=[jax.ShapeDtypeStruct((rows, width // SIDE), F32)] * SIDE,
        scratch_shapes=[pltpu.VMEM((rows, width), F32)],
        compiler_params=params(),
        cost_estimate=about(2),
        name="row_total",
    )(at, *states)


def entering_body(at_ref, *refs):
    ins, outs = refs[:SIDE], refs[SIDE:]
    prefixes(at_ref[0], ins, outs, None)


def prefixes(mine, ins, outs, entering):
    place = [lax.rem(mine - s + SIDE, SIDE) for s in range(SIDE)]
    logs = [ref[D : D + 1, :] for ref in ins]
    for t in range(SIDE):
        if entering is None:
            state = jnp.zeros((D, ins[0].shape[1]), F32)
        else:
            before = sum(flag(place[u] < place[t]) * logs[u] for u in range(SIDE) if u != t)
            state = jnp.exp(before) * entering
        for s in range(SIDE):
            if s == t:
                continue
            gap = sum(
                flag((place[u] > place[s]) & (place[u] < place[t])) * logs[u]
                for u in range(SIDE)
                if u != t and u != s
            )
            state = state + (flag(place[s] < place[t]) * jnp.exp(gap)) * ins[s][:D, :]
        outs[t][...] = state


def entering_rows(at, totals):
    width = totals[0].shape[1]
    return pl.pallas_call(
        entering_body,
        in_specs=[pl.BlockSpec(memory_space=pltpu.SMEM)] + [pl.BlockSpec(memory_space=pltpu.VMEM)] * SIDE,
        out_specs=[pl.BlockSpec(memory_space=pltpu.VMEM)] * SIDE,
        out_shape=[jax.ShapeDtypeStruct((D, width), F32)] * SIDE,
        compiler_params=params(),
        cost_estimate=about(1),
        name="entering_rows",
    )(at, *totals)


def starts_body(at_ref, *refs):
    ins, pieces = refs[:SIDE], refs[SIDE : 2 * SIDE]
    outs, whole = refs[2 * SIDE : 3 * SIDE], refs[3 * SIDE]
    width = pieces[0].shape[1]
    for s in range(SIDE):
        begin = pl.multiple_of(lax.rem(at_ref[0] + s, SIDE) * width, width)
        whole[:, pl.ds(begin, width)] = pieces[s][...]
    prefixes(at_ref[1], ins, outs, whole[...])


def start_states(at, states, entering):
    width = states[0].shape[1]
    return pl.pallas_call(
        starts_body,
        in_specs=[pl.BlockSpec(memory_space=pltpu.SMEM)]
        + [pl.BlockSpec(memory_space=pltpu.VMEM)] * (2 * SIDE),
        out_specs=[pl.BlockSpec(memory_space=pltpu.VMEM)] * SIDE,
        out_shape=[jax.ShapeDtypeStruct((D, width), F32)] * SIDE,
        scratch_shapes=[pltpu.VMEM((D, width), F32)],
        compiler_params=params(),
        cost_estimate=about(2),
        name="start_states",
    )(at, *states, *entering)


def inside_body(at_ref, x_ref, w_ref, r_ref, dt_ref, rate_ref, skip_ref, out_ref, cum, cum_t):
    s = pl.program_id(0)
    rows = dt_ref.shape[1]
    half = rows // 2
    group = lax.rem(at_ref[1] + s, SIDE)

    @pl.when(s == 0)
    def _():
        dt = jnp.transpose(dt_ref[...])
        sums = span_sums(dt * (-jnp.exp(rate_ref[...])), half)
        cum[...] = sums * LOG2E
        cum_t[...] = jnp.transpose((sums - jnp.log(dt)) * LOG2E)

    row = lax.broadcasted_iota(jnp.int32, (half, half), 0)
    col = lax.broadcasted_iota(jnp.int32, (half, half), 1)
    causal = col <= row
    spans = [slice(c * half, (c + 1) * half) for c in range(2)]
    pairs = [row_dot(r_ref[span, :], w_ref[span, :]) for span in spans]

    for g in range(GROUPS):

        @pl.when(group == g)
        def _():
            for j in range(PER):
                h = g * PER + j
                lanes = slice(j * D, (j + 1) * D)
                for c, span in enumerate(spans):
                    x = x_ref[span, lanes]
                    down = jnp.broadcast_to(cum[span, h : h + 1], (half, half))
                    weights = pairs[c] * jnp.exp2(down - cum_t[h : h + 1, span])
                    weights = jnp.where(causal, weights, 0.0).astype(BF)
                    out_ref[span, lanes] = jnp.dot(
                        weights, x, preferred_element_type=F32
                    ) + skip_ref[0, h] * x.astype(F32)


def inside_spans(at, x, w, r, dt, rate, skip):
    rows = x.shape[0]
    width = PER * D

    def turned(s, at):
        return (0, lax.rem(at[1] + s, SIDE))

    def fixed(s, at):
        return (0, 0)

    return pl.pallas_call(
        inside_body,
        grid_spec=pltpu.PrefetchScalarGridSpec(
            num_scalar_prefetch=1,
            grid=(SIDE,),
            in_specs=[
                pl.BlockSpec((rows, width), turned),
                pl.BlockSpec((rows, D), turned),
                pl.BlockSpec((rows, D), turned),
                pl.BlockSpec((SSD_HEADS, rows), fixed),
                pl.BlockSpec((1, SSD_HEADS), fixed),
                pl.BlockSpec(memory_space=pltpu.SMEM),
            ],
            out_specs=pl.BlockSpec((rows, width), turned),
            scratch_shapes=[
                pltpu.VMEM((rows, SSD_HEADS), F32),
                pltpu.VMEM((SSD_HEADS, rows), F32),
            ],
        ),
        out_shape=jax.ShapeDtypeStruct(x.shape, F32),
        compiler_params=params(),
        name="inside_spans",
    )(at, x, w, r, dt, rate, skip)


def ssd_body(
    at_ref, inside_ref, gate_ref, r_ref, dt_ref, rate_ref, gain_ref, sides_ref, ends_ref, *rest
):
    starts, out_hbm, (gated, staged, sems) = rest[:SIDE], rest[SIDE], rest[SIDE + 1 :]
    firsts = {1: sides_ref.at[0], 3: sides_ref.at[1], 2: ends_ref.at[0], 0: ends_ref.at[1]}
    y = at_ref[1]
    rows = dt_ref.shape[1]
    half = rows // 2
    width = PER * D
    sums = span_sums(jnp.transpose(dt_ref[...]) * (-jnp.exp(rate_ref[...])), half)
    ends = jnp.broadcast_to(sums[half - 1 : half], (8, SSD_HEADS))
    copies = []
    for s in (0, 1, 3, 2):
        group = lax.rem(y + s, SIDE)
        turn = SSD_HEADS - PER * group
        grown, decay = [
            jnp.exp(pltpu.roll(jnp.concatenate([part] * (D // SSD_HEADS), axis=1), turn, 1))
            for part in (sums, ends)
        ]
        decay = jnp.concatenate(
            [jnp.broadcast_to(decay[0:1, j : j + 1], (1, D)) for j in range(PER)], axis=1
        )
        read = r_ref[:, columns(group, D)]
        start = starts[s][...]
        gated[:half, :] = jnp.dot(read[:half], start.astype(BF), preferred_element_type=F32)
        gated[half:, :] = jnp.dot(
            read[half:], (decay * start + firsts[s][...]).astype(BF), preferred_element_type=F32
        )
        square = jnp.zeros((rows, D), F32)
        for j in range(PER):
            lanes = slice(j * D, (j + 1) * D)
            there = columns(group * PER + j, D)
            mixed = inside_ref[:, there] + grown[:, j : j + 1] * gated[:, lanes]
            gate = gate_ref[:, there].astype(F32)
            value = mixed * (gate * (0.5 + 0.5 * jnp.tanh(0.5 * gate)))
            gated[:, lanes] = value
            square = square + value * value
        mean = jnp.sum(square, axis=1, keepdims=True) * (1.0 / width)
        inverse = lax.rsqrt(mean + 1e-05)
        for j in range(PER):
            lanes = slice(j * D, (j + 1) * D)
            there = columns(group * PER + j, D)
            staged[s, :, lanes] = (
                gated[:, lanes] * inverse * gain_ref[:, there].astype(F32)
            ).astype(BF)
        copy = pltpu.make_async_copy(
            staged.at[s], out_hbm.at[:, columns(group, width)], sems.at[s]
        )
        copy.start()
        copies.append(copy)
    for copy in copies:
        copy.wait()


def ssd_out_of(at, inside, gate, r, dt, rate, gain, first, starts):
    rows = inside.shape[0]
    width = PER * D
    near = pl.BlockSpec(memory_space=pltpu.VMEM)
    return pl.pallas_call(
        ssd_body,
        in_specs=[pl.BlockSpec(memory_space=pltpu.SMEM)] + [near] * (8 + SIDE),
        out_specs=pl.BlockSpec(memory_space=pltpu.HBM),
        scratch_shapes=[
            pltpu.VMEM((rows, width), F32),
            pltpu.VMEM((SIDE, rows, width), BF),
            pltpu.SemaphoreType.DMA((SIDE,)),
        ],
        out_shape=jax.ShapeDtypeStruct(gate.shape, BF),
        compiler_params=params(24),
        cost_estimate=about(8),
        name="ssd_out",
    )(at, inside, gate, r, dt, rate, gain, *first, *starts)


def load_queries(q_ref, qs):
    rows = q_ref.shape[0]
    for h in range(NQ):
        qs[h * rows : (h + 1) * rows, :] = q_ref[:, (2 + h) * D : (3 + h) * D]


def row_dot(a, b):
    return lax.dot_general(a, b, (((1,), (1,)), ((), ())), preferred_element_type=F32)


def lane_max(scores):
    return jnp.maximum(scores[:, :D], scores[:, D:])


def spread_max(parts):
    most = parts[0]
    for part in parts[1:]:
        most = jnp.maximum(most, part)
    return jnp.broadcast_to(jnp.max(most, axis=1, keepdims=True), most.shape)


def attention_body(at_ref, *rest):
    pieces, parts, outs = rest[:SIDE], rest[SIDE : 2 * SIDE], rest[2 * SIDE : 3 * SIDE]
    qs, acc, top = rest[3 * SIDE :]
    place = pl.program_id(0)
    x, y = at_ref[0], at_ref[1]
    rows = pieces[0].shape[0]
    ones = jnp.ones((rows, D), BF)

    for s in range(SIDE):

        @pl.when(lax.rem(x - place + SIDE, SIDE) == s)
        def _():
            load_queries(pieces[s], qs)

    acc[...] = jnp.zeros_like(acc)
    top[...] = jnp.full_like(top, NEG)

    def chunk(c, newest):
        where = pl.ds(pl.multiple_of(lax.rem(x - c + SIDE, SIDE) * rows, rows), rows)
        if newest:
            causal = lax.broadcasted_iota(jnp.int32, (rows, rows), 1) <= lax.broadcasted_iota(
                jnp.int32, (rows, rows), 0
            )
            shown = [0.0] + [
                jnp.where(lax.rem(y - u + SIDE, SIDE) > y, NEG, 0.0).astype(F32)
                for u in range(1, SIDE)
            ]

        def scores(h):
            mine = qs[h * 2 * rows : (h + 1) * 2 * rows, :]
            found = [row_dot(mine, part[where, :D]) for part in parts]
            if newest:
                found[0] = jnp.where(jnp.concatenate([causal, causal], axis=0), found[0], NEG)
            return found

        now = scores(0)
        for h in range(NQ // 2):
            following = scores(h + 1) if h + 1 < NQ // 2 else None
            mine = slice(h * 2 * rows, (h + 1) * 2 * rows)
            old = top[mine, :]
            most = [lane_max(part) for part in now]
            if newest:
                most = [part + shift for part, shift in zip(most, shown)]
            new = jnp.maximum(old, spread_max(most))
            wide = jnp.concatenate([new] * (rows // D), axis=1)
            factor = jnp.exp2((old - new) * SCALE)
            top[mine, :] = new
            out = acc[mine, :] * jnp.concatenate([factor, factor], axis=1)
            for u in range(SIDE):
                base = wide - shown[u] if newest and u else wide
                weights = jnp.exp2((now[u] - base) * SCALE).astype(BF)
                values = jnp.concatenate([parts[u][where, D:], ones], axis=1)
                out = out + jnp.dot(weights, values, preferred_element_type=F32)
            acc[mine, :] = out
            now = following

    def older(c, carry):
        chunk(c, False)
        return carry

    lax.fori_loop(0, place, older, 0)
    chunk(place, True)
    for s in range(SIDE):

        @pl.when(lax.rem(x - place + SIDE, SIDE) == s)
        def _():
            for h in range(NQ):
                mine = slice(h * rows, (h + 1) * rows)
                outs[s][:, h * D : (h + 1) * D] = (acc[mine, :D] / acc[mine, D:]).astype(BF)


def attention(at, pieces, parts):
    rows, width = pieces[0].shape
    given = width - 2 * D

    near = pl.BlockSpec(memory_space=pltpu.VMEM)

    return pl.pallas_call(
        attention_body,
        grid_spec=pltpu.PrefetchScalarGridSpec(
            num_scalar_prefetch=1,
            grid=(SIDE,),
            in_specs=[near] * (2 * SIDE),
            out_specs=[near] * SIDE,
            scratch_shapes=[
                pltpu.VMEM((NQ * rows, D), BF),
                pltpu.VMEM((NQ * rows, 2 * D), F32),
                pltpu.VMEM((NQ * rows, D), F32),
            ],
        ),
        out_shape=[jax.ShapeDtypeStruct((rows, given), BF)] * SIDE,
        compiler_params=params(28),
        cost_estimate=about(18),
        name="attention",
    )(at, *pieces, *parts)


def unpack_body(at_ref, *refs):
    ins, out, sems = refs[:SIDE], refs[SIDE], refs[SIDE + 1]
    width = ins[0].shape[1]
    copies = [
        pltpu.make_async_copy(
            ins[s], out.at[:, columns(lax.rem(at_ref[0] + s, SIDE), width)], sems.at[s]
        )
        for s in range(SIDE)
    ]
    for copy in copies:
        copy.start()
    for copy in copies:
        copy.wait()


def unpack(at, pieces):
    rows, width = pieces[0].shape
    return pl.pallas_call(
        unpack_body,
        in_specs=[pl.BlockSpec(memory_space=pltpu.SMEM)]
        + [pl.BlockSpec(memory_space=pltpu.VMEM)] * SIDE,
        out_specs=pl.BlockSpec(memory_space=pltpu.HBM),
        out_shape=jax.ShapeDtypeStruct((rows, SIDE * width), BF),
        scratch_shapes=[pltpu.SemaphoreType.DMA((SIDE,))],
        compiler_params=params(),
        cost_estimate=about(2),
        name="unpack",
    )(at, *pieces)


def shifted(value, axis, by):
    return lax.ppermute(value, axis, [(i, (i + by) % SIDE) for i in range(SIDE)])


def exchange(pieces, axis, sign):
    return [pieces[0]] + [shifted(pieces[s], axis, sign * s) for s in range(1, SIDE)]


def local(
    ssd_input, gate_input, write_map, read_map, step_size, decay_log, skip_gain, norm_gain,
    query_rows, key_rows, value_rows,
):
    step_size = step_size.T
    at = jnp.stack([lax.axis_index("x"), lax.axis_index("y")]).astype(jnp.int32)
    rate = decay_log.reshape(1, -1)
    skip = skip_gain.reshape(1, -1)
    gain = norm_gain.reshape(1, -1)
    tie = lax.optimization_barrier
    given = (ssd_input, write_map, step_size, rate)
    one, three, sides = local_states(at, (1, 3), *given)
    one, three, given, packed = tie((one, three, given, (key_rows, value_rows, query_rows)))
    two, mine, rest = local_states(at, (2, 0), *given)
    first = [sides, rest]
    states = exchange([mine, one, two, three], "y", 1)
    pieces = exchange(pack(at, *packed), "x", 1)
    inside = inside_spans(at, ssd_input, write_map, read_map, step_size, rate, skip)
    pieces, inside = tie((pieces, inside))
    own = stack(pieces)
    middle = own.shape[0] // 2
    before = shifted(own, "y", 1)
    after = shifted(own, "y", -1)
    states, inside = tie((states, inside))
    totals = exchange(row_total(at, states), "x", 1)
    entering = entering_rows(at, totals)
    entering, before, after = tie((entering, before, after))
    far = [shifted(before[:middle], "y", 1), shifted(after[middle:], "y", -1)]
    entering = exchange(entering, "x", -1)
    starts = start_states(at, states, entering)
    starts, pieces = tie((starts, pieces))
    starts = exchange(starts, "y", -1)
    parts = [own, before, jnp.concatenate(far, axis=0), after]
    back = exchange(attention(at, pieces, parts), "x", -1)
    ssd = ssd_out_of(at, inside, gate_input, read_map, step_size, rate, gain, first, starts)
    ssd, back = tie((ssd, back))
    return (ssd, unpack(at, back))


def solution(mesh):
    grid = Mesh(mesh.devices.reshape(-1, SIDE, SIDE), ("dp", "x", "y"))
    split = P(("dp", "x", "y"), None)
    in_specs = (split,) * 5 + (P(), P(), P()) + (split,) * 3
    return jax.shard_map(
        local, mesh=grid, in_specs=in_specs, out_specs=(split, split), check_vma=False
    )
```

```python
import functools
import math

import jax
import jax.numpy as jnp
from jax import lax
from jax.experimental import pallas as pl
from jax.experimental.pallas import tpu as pltpu
from jax.sharding import Mesh, PartitionSpec as P

SSD_HEADS = 32
GROUPS = 4
PER = SSD_HEADS // GROUPS
D = 128
NQ = 4
KV_HEADS = 4
SIDE = 4
SCALE = (D**-0.5) * math.log2(math.e)
LOG2E = math.log2(math.e)
BF = jnp.bfloat16
F32 = jnp.float32
NEG = -1e30
EXTRA = 8


def params(mib=16):
    return pltpu.CompilerParams(vmem_limit_bytes=mib << 20)


def about(us):
    return pl.CostEstimate(
        flops=int(us * 1.0e9), bytes_accessed=int(us * 3.0e6), transcendentals=0
    )


def columns(begin, width):
    return pl.ds(pl.multiple_of(begin * width, D), width)


def pack_body(at_ref, *refs):
    outs = refs[3 * SIDE :]
    for s in range(SIDE):
        outs[s][:, :D] = refs[3 * s][...]
        outs[s][:, D : 2 * D] = refs[3 * s + 1][...]
        outs[s][:, 2 * D :] = refs[3 * s + 2][...]


def pack(at, k, v, q):
    rows, cols = q.shape
    width = cols // SIDE

    def spec(s, width):
        return pl.BlockSpec((rows, width), lambda g, at: (0, lax.rem(at[0] + s, SIDE)))

    return pl.pallas_call(
        pack_body,
        grid_spec=pltpu.PrefetchScalarGridSpec(
            num_scalar_prefetch=1,
            grid=(1,),
            in_specs=[spec(s, w) for s in range(SIDE) for w in (D, D, width)],
            out_specs=[pl.BlockSpec((rows, 2 * D + width), lambda g, at: (0, 0))] * SIDE,
        ),
        out_shape=[jax.ShapeDtypeStruct((rows, 2 * D + width), BF)] * SIDE,
        compiler_params=params(),
        name="pack",
    )(at, *([k, v, q] * SIDE))


def stack_body(*refs):
    ins, out = refs[:SIDE], refs[SIDE]
    rows = ins[0].shape[0]
    for s in range(SIDE):
        out[s * rows : (s + 1) * rows, :] = ins[s][...]


def stack(pieces):
    rows = pieces[0].shape[0]
    return pl.pallas_call(
        stack_body,
        grid=(1,),
        in_specs=[pl.BlockSpec((rows, 2 * D), lambda g: (0, 0))] * SIDE,
        out_specs=pl.BlockSpec((SIDE * rows, 2 * D), lambda g: (0, 0)),
        out_shape=jax.ShapeDtypeStruct((SIDE * rows, 2 * D), BF),
        compiler_params=params(),
        name="stack",
    )(*pieces)


def span_sums(log_decay, span):
    row = lax.rem(lax.broadcasted_iota(jnp.int32, log_decay.shape, 0), span)
    step = 1
    while step < span:
        moved = pltpu.roll(log_decay, step, 0)
        log_decay = log_decay + jnp.where(row >= step, moved, 0.0)
        step *= 2
    return log_decay


def state_body(slots, at_ref, x_hbm, w_hbm, dt_hbm, rate_hbm, *rest):
    n = len(slots)
    outs, first_ref, (x_ref, w_ref, dt_ref, rate_ref, sems) = rest[:n], rest[n], rest[n + 1 :]
    rows = dt_ref.shape[1]
    half = rows // 2
    width = PER * D
    y = at_ref[1]
    steps = pltpu.make_async_copy(dt_hbm, dt_ref, sems.at[2 * n])
    steps.start()
    rates = pltpu.make_async_copy(rate_hbm, rate_ref, sems.at[2 * n + 1])
    rates.start()
    arrivals = []
    for i, s in enumerate(slots):
        group = lax.rem(y + s, SIDE)
        arrivals.append(
            (
                i,
                s,
                pltpu.make_async_copy(
                    w_hbm.at[:, columns(group, D)], w_ref.at[i], sems.at[n + i]
                ),
                pltpu.make_async_copy(
                    x_hbm.at[:, columns(group, width)], x_ref.at[i], sems.at[i]
                ),
            )
        )
    for _, _, w_copy, x_copy in arrivals:
        w_copy.start()
        x_copy.start()
    steps.wait()
    rates.wait()
    dt = jnp.transpose(dt_ref[...])
    sums = span_sums(dt * (-jnp.exp(rate_ref[...])), half)
    ends = jnp.concatenate(
        [jnp.broadcast_to(sums[half * c + half - 1 : half * c + half], (half, SSD_HEADS)) for c in range(2)],
        axis=0,
    )
    to_end = jnp.exp(ends - sums) * dt
    last = ends[half : half + 8]
    total = ends[:8] + last
    for i, s, w_copy, x_copy in arrivals:
        turn = SSD_HEADS - PER * lax.rem(y + s, SIDE)
        mine, last_mine, total_mine = [
            pltpu.roll(jnp.concatenate([part] * (D // SSD_HEADS), axis=1), turn, 1)
            for part in (to_end, last, total)
        ]
        w_copy.wait()
        x_copy.wait()
        scaled = jnp.concatenate(
            [
                (mine[:, j : j + 1] * x_ref[i, :, j * D : (j + 1) * D].astype(F32)).astype(BF)
                for j in range(PER)
            ],
            axis=1,
        )
        first, second = [
            lax.dot_general(
                w_ref[i, c * half : (c + 1) * half, :],
                scaled[c * half : (c + 1) * half],
                (((0,), (0,)), ((), ())),
                preferred_element_type=F32,
            )
            for c in range(2)
        ]
        first_ref[i] = first
        decay = jnp.concatenate(
            [jnp.broadcast_to(last_mine[0:1, j : j + 1], (1, D)) for j in range(PER)], axis=1
        )
        outs[i][:D, :] = jnp.exp(decay) * first + second
        outs[i][D:, :] = jnp.concatenate(
            [jnp.broadcast_to(total_mine[:, j : j + 1], (EXTRA, D)) for j in range(PER)], axis=1
        )


def local_states(at, slots, x, w, dt, rate):
    n = len(slots)
    rows = x.shape[0]
    width = PER * D
    far = pl.BlockSpec(memory_space=pltpu.HBM)
    near = pl.BlockSpec(memory_space=pltpu.VMEM)
    return pl.pallas_call(
        functools.partial(state_body, slots),
        in_specs=[pl.BlockSpec(memory_space=pltpu.SMEM), far, far, far, far],
        out_specs=[near] * (n + 1),
        scratch_shapes=[
            pltpu.VMEM((n, rows, width), BF),
            pltpu.VMEM((n, rows, D), BF),
            pltpu.VMEM((SSD_HEADS, rows), F32),
            pltpu.VMEM((1, SSD_HEADS), F32),
            pltpu.SemaphoreType.DMA((2 * n + 2,)),
        ],
        out_shape=[jax.ShapeDtypeStruct((D + EXTRA, width), F32)] * n
        + [jax.ShapeDtypeStruct((n, D, width), F32)],
        compiler_params=params(),
        name="local_states",
    )(at, *[pltpu.with_memory_space_constraint(part, pltpu.HBM) for part in (x, w, dt, rate)])


def flag(condition):
    return jnp.where(condition, 1.0, 0.0).astype(F32)


def row_total_body(at_ref, *refs):
    ins, outs, total = refs[:SIDE], refs[SIDE : 2 * SIDE], refs[2 * SIDE]
    x, y = at_ref[0], at_ref[1]
    place = [lax.rem(y - s + SIDE, SIDE) for s in range(SIDE)]
    logs = [ref[D : D + 1, :] for ref in ins]
    value = None
    for s in range(SIDE):
        later = sum(flag(place[u] > place[s]) * logs[u] for u in range(SIDE) if u != s)
        term = ins[s][:D, :] * jnp.exp(later)
        value = term if value is None else value + term
    total[:D, :] = value
    total[D:, :] = jnp.broadcast_to(logs[0] + logs[1] + logs[2] + logs[3], (EXTRA, value.shape[1]))
    width = value.shape[1] // SIDE
    for s in range(SIDE):
        begin = pl.multiple_of(lax.rem(x + s, SIDE) * width, width)
        outs[s][...] = total[:, pl.ds(begin, width)]


def row_total(at, states):
    rows, width = states[0].shape
    return pl.pallas_call(
        row_total_body,
        in_specs=[pl.BlockSpec(memory_space=pltpu.SMEM)] + [pl.BlockSpec(memory_space=pltpu.VMEM)] * SIDE,
        out_specs=[pl.BlockSpec(memory_space=pltpu.VMEM)] * SIDE,
        out_shape=[jax.ShapeDtypeStruct((rows, width // SIDE), F32)] * SIDE,
        scratch_shapes=[pltpu.VMEM((rows, width), F32)],
        compiler_params=params(),
        cost_estimate=about(2),
        name="row_total",
    )(at, *states)


def entering_body(at_ref, *refs):
    ins, outs = refs[:SIDE], refs[SIDE:]
    prefixes(at_ref[0], ins, outs, None)


def prefixes(mine, ins, outs, entering):
    place = [lax.rem(mine - s + SIDE, SIDE) for s in range(SIDE)]
    logs = [ref[D : D + 1, :] for ref in ins]
    for t in range(SIDE):
        if entering is None:
            state = jnp.zeros((D, ins[0].shape[1]), F32)
        else:
            before = sum(flag(place[u] < place[t]) * logs[u] for u in range(SIDE) if u != t)
            state = jnp.exp(before) * entering
        for s in range(SIDE):
            if s == t:
                continue
            gap = sum(
                flag((place[u] > place[s]) & (place[u] < place[t])) * logs[u]
                for u in range(SIDE)
                if u != t and u != s
            )
            state = state + (flag(place[s] < place[t]) * jnp.exp(gap)) * ins[s][:D, :]
        outs[t][...] = state


def entering_rows(at, totals):
    width = totals[0].shape[1]
    return pl.pallas_call(
        entering_body,
        in_specs=[pl.BlockSpec(memory_space=pltpu.SMEM)] + [pl.BlockSpec(memory_space=pltpu.VMEM)] * SIDE,
        out_specs=[pl.BlockSpec(memory_space=pltpu.VMEM)] * SIDE,
        out_shape=[jax.ShapeDtypeStruct((D, width), F32)] * SIDE,
        compiler_params=params(),
        cost_estimate=about(1),
        name="entering_rows",
    )(at, *totals)


def starts_body(at_ref, *refs):
    ins, pieces = refs[:SIDE], refs[SIDE : 2 * SIDE]
    outs, whole = refs[2 * SIDE : 3 * SIDE], refs[3 * SIDE]
    width = pieces[0].shape[1]
    for s in range(SIDE):
        begin = pl.multiple_of(lax.rem(at_ref[0] + s, SIDE) * width, width)
        whole[:, pl.ds(begin, width)] = pieces[s][...]
    prefixes(at_ref[1], ins, outs, whole[...])


def start_states(at, states, entering):
    width = states[0].shape[1]
    return pl.pallas_call(
        starts_body,
        in_specs=[pl.BlockSpec(memory_space=pltpu.SMEM)]
        + [pl.BlockSpec(memory_space=pltpu.VMEM)] * (2 * SIDE),
        out_specs=[pl.BlockSpec(memory_space=pltpu.VMEM)] * SIDE,
        out_shape=[jax.ShapeDtypeStruct((D, width), F32)] * SIDE,
        scratch_shapes=[pltpu.VMEM((D, width), F32)],
        compiler_params=params(),
        cost_estimate=about(2),
        name="start_states",
    )(at, *states, *entering)


def inside_body(at_ref, x_ref, w_ref, r_ref, dt_ref, rate_ref, skip_ref, out_ref, cum, cum_t):
    s = pl.program_id(0)
    rows = dt_ref.shape[1]
    half = rows // 2
    group = lax.rem(at_ref[1] + s, SIDE)

    @pl.when(s == 0)
    def _():
        dt = jnp.transpose(dt_ref[...])
        sums = span_sums(dt * (-jnp.exp(rate_ref[...])), half)
        cum[...] = sums * LOG2E
        cum_t[...] = jnp.transpose((sums - jnp.log(dt)) * LOG2E)

    row = lax.broadcasted_iota(jnp.int32, (half, half), 0)
    col = lax.broadcasted_iota(jnp.int32, (half, half), 1)
    causal = col <= row
    spans = [slice(c * half, (c + 1) * half) for c in range(2)]
    pairs = [row_dot(r_ref[span, :], w_ref[span, :]) for span in spans]

    for g in range(GROUPS):

        @pl.when(group == g)
        def _():
            for j in range(PER):
                h = g * PER + j
                lanes = slice(j * D, (j + 1) * D)
                for c, span in enumerate(spans):
                    x = x_ref[span, lanes]
                    down = jnp.broadcast_to(cum[span, h : h + 1], (half, half))
                    weights = pairs[c] * jnp.exp2(down - cum_t[h : h + 1, span])
                    weights = jnp.where(causal, weights, 0.0).astype(BF)
                    out_ref[span, lanes] = jnp.dot(
                        weights, x, preferred_element_type=F32
                    ) + skip_ref[0, h] * x.astype(F32)


def inside_spans(at, x, w, r, dt, rate, skip):
    rows = x.shape[0]
    width = PER * D

    def turned(s, at):
        return (0, lax.rem(at[1] + s, SIDE))

    def fixed(s, at):
        return (0, 0)

    return pl.pallas_call(
        inside_body,
        grid_spec=pltpu.PrefetchScalarGridSpec(
            num_scalar_prefetch=1,
            grid=(SIDE,),
            in_specs=[
                pl.BlockSpec((rows, width), turned),
                pl.BlockSpec((rows, D), turned),
                pl.BlockSpec((rows, D), turned),
                pl.BlockSpec((SSD_HEADS, rows), fixed),
                pl.BlockSpec((1, SSD_HEADS), fixed),
                pl.BlockSpec(memory_space=pltpu.SMEM),
            ],
            out_specs=pl.BlockSpec((rows, width), turned),
            scratch_shapes=[
                pltpu.VMEM((rows, SSD_HEADS), F32),
                pltpu.VMEM((SSD_HEADS, rows), F32),
            ],
        ),
        out_shape=jax.ShapeDtypeStruct(x.shape, F32),
        compiler_params=params(),
        name="inside_spans",
    )(at, x, w, r, dt, rate, skip)


def ssd_body(
    at_ref, inside_ref, gate_ref, r_ref, dt_ref, rate_ref, gain_ref, sides_ref, ends_ref, *rest
):
    starts, out_hbm, (gated, staged, sems) = rest[:SIDE], rest[SIDE], rest[SIDE + 1 :]
    firsts = {1: sides_ref.at[0], 3: sides_ref.at[1], 2: ends_ref.at[0], 0: ends_ref.at[1]}
    y = at_ref[1]
    rows = dt_ref.shape[1]
    half = rows // 2
    width = PER * D
    sums = span_sums(jnp.transpose(dt_ref[...]) * (-jnp.exp(rate_ref[...])), half)
    ends = jnp.broadcast_to(sums[half - 1 : half], (8, SSD_HEADS))
    copies = []
    for s in (0, 1, 3, 2):
        group = lax.rem(y + s, SIDE)
        turn = SSD_HEADS - PER * group
        grown, decay = [
            jnp.exp(pltpu.roll(jnp.concatenate([part] * (D // SSD_HEADS), axis=1), turn, 1))
            for part in (sums, ends)
        ]
        decay = jnp.concatenate(
            [jnp.broadcast_to(decay[0:1, j : j + 1], (1, D)) for j in range(PER)], axis=1
        )
        read = r_ref[:, columns(group, D)]
        start = starts[s][...]
        gated[:half, :] = jnp.dot(read[:half], start.astype(BF), preferred_element_type=F32)
        gated[half:, :] = jnp.dot(
            read[half:], (decay * start + firsts[s][...]).astype(BF), preferred_element_type=F32
        )
        square = jnp.zeros((rows, D), F32)
        for j in range(PER):
            lanes = slice(j * D, (j + 1) * D)
            there = columns(group * PER + j, D)
            mixed = inside_ref[:, there] + grown[:, j : j + 1] * gated[:, lanes]
            gate = gate_ref[:, there].astype(F32)
            value = mixed * (gate * (0.5 + 0.5 * jnp.tanh(0.5 * gate)))
            gated[:, lanes] = value
            square = square + value * value
        mean = jnp.sum(square, axis=1, keepdims=True) * (1.0 / width)
        inverse = lax.rsqrt(mean + 1e-05)
        for j in range(PER):
            lanes = slice(j * D, (j + 1) * D)
            there = columns(group * PER + j, D)
            staged[s, :, lanes] = (
                gated[:, lanes] * inverse * gain_ref[:, there].astype(F32)
            ).astype(BF)
        copy = pltpu.make_async_copy(
            staged.at[s], out_hbm.at[:, columns(group, width)], sems.at[s]
        )
        copy.start()
        copies.append(copy)
    for copy in copies:
        copy.wait()


def ssd_out_of(at, inside, gate, r, dt, rate, gain, first, starts):
    rows = inside.shape[0]
    width = PER * D
    near = pl.BlockSpec(memory_space=pltpu.VMEM)
    return pl.pallas_call(
        ssd_body,
        in_specs=[pl.BlockSpec(memory_space=pltpu.SMEM)] + [near] * (8 + SIDE),
        out_specs=pl.BlockSpec(memory_space=pltpu.HBM),
        scratch_shapes=[
            pltpu.VMEM((rows, width), F32),
            pltpu.VMEM((SIDE, rows, width), BF),
            pltpu.SemaphoreType.DMA((SIDE,)),
        ],
        out_shape=jax.ShapeDtypeStruct(gate.shape, BF),
        compiler_params=params(24),
        cost_estimate=about(8),
        name="ssd_out",
    )(at, inside, gate, r, dt, rate, gain, *first, *starts)


def load_queries(q_ref, qs):
    rows = q_ref.shape[0]
    for h in range(NQ):
        qs[h * rows : (h + 1) * rows, :] = q_ref[:, (2 + h) * D : (3 + h) * D]


def row_dot(a, b):
    return lax.dot_general(a, b, (((1,), (1,)), ((), ())), preferred_element_type=F32)


def lane_max(scores):
    return jnp.maximum(scores[:, :D], scores[:, D:])


def spread_max(parts):
    most = parts[0]
    for part in parts[1:]:
        most = jnp.maximum(most, part)
    return jnp.broadcast_to(jnp.max(most, axis=1, keepdims=True), most.shape)


def attention_body(at_ref, *rest):
    pieces, parts, outs = rest[:SIDE], rest[SIDE : 2 * SIDE], rest[2 * SIDE : 3 * SIDE]
    qs, acc, top = rest[3 * SIDE :]
    place = pl.program_id(0)
    x, y = at_ref[0], at_ref[1]
    rows = pieces[0].shape[0]
    ones = jnp.ones((rows, D), BF)

    for s in range(SIDE):

        @pl.when(lax.rem(x - place + SIDE, SIDE) == s)
        def _():
            load_queries(pieces[s], qs)

    acc[...] = jnp.zeros_like(acc)
    top[...] = jnp.full_like(top, NEG)

    def chunk(c, newest):
        where = pl.ds(pl.multiple_of(lax.rem(x - c + SIDE, SIDE) * rows, rows), rows)
        if newest:
            causal = lax.broadcasted_iota(jnp.int32, (rows, rows), 1) <= lax.broadcasted_iota(
                jnp.int32, (rows, rows), 0
            )
            shown = [0.0] + [
                jnp.where(lax.rem(y - u + SIDE, SIDE) > y, NEG, 0.0).astype(F32)
                for u in range(1, SIDE)
            ]

        def scores(h):
            mine = qs[h * 2 * rows : (h + 1) * 2 * rows, :]
            found = [row_dot(mine, part[where, :D]) for part in parts]
            if newest:
                found[0] = jnp.where(jnp.concatenate([causal, causal], axis=0), found[0], NEG)
            return found

        now = scores(0)
        for h in range(NQ // 2):
            following = scores(h + 1) if h + 1 < NQ // 2 else None
            mine = slice(h * 2 * rows, (h + 1) * 2 * rows)
            old = top[mine, :]
            most = [lane_max(part) for part in now]
            if newest:
                most = [part + shift for part, shift in zip(most, shown)]
            new = jnp.maximum(old, spread_max(most))
            wide = jnp.concatenate([new] * (rows // D), axis=1)
            factor = jnp.exp2((old - new) * SCALE)
            top[mine, :] = new
            out = acc[mine, :] * jnp.concatenate([factor, factor], axis=1)
            for u in range(SIDE):
                base = wide - shown[u] if newest and u else wide
                weights = jnp.exp2((now[u] - base) * SCALE).astype(BF)
                values = jnp.concatenate([parts[u][where, D:], ones], axis=1)
                out = out + jnp.dot(weights, values, preferred_element_type=F32)
            acc[mine, :] = out
            now = following

    def older(c, carry):
        chunk(c, False)
        return carry

    lax.fori_loop(0, place, older, 0)
    chunk(place, True)
    for s in range(SIDE):

        @pl.when(lax.rem(x - place + SIDE, SIDE) == s)
        def _():
            for h in range(NQ):
                mine = slice(h * rows, (h + 1) * rows)
                outs[s][:, h * D : (h + 1) * D] = (acc[mine, :D] / acc[mine, D:]).astype(BF)


def attention(at, pieces, parts):
    rows, width = pieces[0].shape
    given = width - 2 * D

    near = pl.BlockSpec(memory_space=pltpu.VMEM)

    return pl.pallas_call(
        attention_body,
        grid_spec=pltpu.PrefetchScalarGridSpec(
            num_scalar_prefetch=1,
            grid=(SIDE,),
            in_specs=[near] * (2 * SIDE),
            out_specs=[near] * SIDE,
            scratch_shapes=[
                pltpu.VMEM((NQ * rows, D), BF),
                pltpu.VMEM((NQ * rows, 2 * D), F32),
                pltpu.VMEM((NQ * rows, D), F32),
            ],
        ),
        out_shape=[jax.ShapeDtypeStruct((rows, given), BF)] * SIDE,
        compiler_params=params(28),
        cost_estimate=about(18),
        name="attention",
    )(at, *pieces, *parts)


def unpack_body(at_ref, *refs):
    ins, out, sems = refs[:SIDE], refs[SIDE], refs[SIDE + 1]
    width = ins[0].shape[1]
    copies = [
        pltpu.make_async_copy(
            ins[s], out.at[:, columns(lax.rem(at_ref[0] + s, SIDE), width)], sems.at[s]
        )
        for s in range(SIDE)
    ]
    for copy in copies:
        copy.start()
    for copy in copies:
        copy.wait()


def unpack(at, pieces):
    rows, width = pieces[0].shape
    return pl.pallas_call(
        unpack_body,
        in_specs=[pl.BlockSpec(memory_space=pltpu.SMEM)]
        + [pl.BlockSpec(memory_space=pltpu.VMEM)] * SIDE,
        out_specs=pl.BlockSpec(memory_space=pltpu.HBM),
        out_shape=jax.ShapeDtypeStruct((rows, SIDE * width), BF),
        scratch_shapes=[pltpu.SemaphoreType.DMA((SIDE,))],
        compiler_params=params(),
        cost_estimate=about(2),
        name="unpack",
    )(at, *pieces)


def shifted(value, axis, by):
    return lax.ppermute(value, axis, [(i, (i + by) % SIDE) for i in range(SIDE)])


def exchange(pieces, axis, sign):
    return [pieces[0]] + [shifted(pieces[s], axis, sign * s) for s in range(1, SIDE)]


def local(
    ssd_input, gate_input, write_map, read_map, step_size, decay_log, skip_gain, norm_gain,
    query_rows, key_rows, value_rows,
):
    step_size = step_size.T
    at = jnp.stack([lax.axis_index("x"), lax.axis_index("y")]).astype(jnp.int32)
    rate = decay_log.reshape(1, -1)
    skip = skip_gain.reshape(1, -1)
    gain = norm_gain.reshape(1, -1)
    tie = lax.optimization_barrier
    given = (ssd_input, write_map, step_size, rate)
    one, three, sides = local_states(at, (1, 3), *given)
    one, three, given, packed = tie((one, three, given, (key_rows, value_rows, query_rows)))
    two, mine, rest = local_states(at, (2, 0), *given)
    first = [sides, rest]
    pieces = list(pack(at, *packed))
    two, pieces[1], pieces[3] = tie((two, pieces[1], pieces[3]))
    states = exchange([mine, one, two, three], "y", 1)
    pieces = exchange(pieces, "x", 1)
    inside = inside_spans(at, ssd_input, write_map, read_map, step_size, rate, skip)
    pieces, inside = tie((pieces, inside))
    own = stack(pieces)
    middle = own.shape[0] // 2
    before = shifted(own, "y", 1)
    after = shifted(own, "y", -1)
    states, inside = tie((states, inside))
    totals = exchange(row_total(at, states), "x", 1)
    entering = entering_rows(at, totals)
    entering, before, after = tie((entering, before, after))
    far = [shifted(before[:middle], "y", 1), shifted(after[middle:], "y", -1)]
    entering = exchange(entering, "x", -1)
    starts = start_states(at, states, entering)
    starts, pieces = tie((starts, pieces))
    starts = exchange(starts, "y", -1)
    parts = [own, before, jnp.concatenate(far, axis=0), after]
    back = exchange(attention(at, pieces, parts), "x", -1)
    ssd = ssd_out_of(at, inside, gate_input, read_map, step_size, rate, gain, first, starts)
    ssd, back = tie((ssd, back))
    return (ssd, unpack(at, back))


def solution(mesh):
    grid = Mesh(mesh.devices.reshape(-1, SIDE, SIDE), ("dp", "x", "y"))
    split = P(("dp", "x", "y"), None)
    in_specs = (split,) * 5 + (P(), P(), P()) + (split,) * 3
    return jax.shard_map(
        local, mesh=grid, in_specs=in_specs, out_specs=(split, split), check_vma=False
    )
```
